128 devices in a mesh: region: 4 (over x), wave: 32 (over y, z, core).
Axes of the slice: x: 4, y: 4, z: 4, core: 2. Of those that a mesh axis runs over, the one named last changes fastest.
Arguments:
- state0: float32 [9, 35, 32768], P(None, None, ('region', 'wave')), may hold values from -6 to 6
- delta: float32 [9, 35, 32768], P(None, None, ('region', 'wave')), may hold values from -6 to 6
- adjoint: float32 [9, 35, 32768], P(None, None, ('region', 'wave')), may hold values from -6 to 6
- model: float32 [3, 35, 32768], P(None, None, ('region', 'wave')), may hold values from 0.5 to 2
- geometry: float32 [9, 32768], P(None, ('region', 'wave')), may hold values from -4 to 4
- normals: float32 [3, 4, 32768], P(None, None, ('region', 'wave')), may hold values from -1 to 1
- face_scale: float32 [4, 32768], P(None, ('region', 'wave')), may hold values from 0.5 to 2
- derivative: float32 [3, 35, 35], replicated, may hold values from -1 to 1
- lift: float32 [4, 35, 15], replicated, may hold values from -1.5 to 1.5
- prolong: float32 [8, 35, 10], replicated, may hold values from -2 to 2
- coarse_step: float32 [30, 4096], P(None, ('region', 'wave')), may hold values from -6 to 6
- reg_weight: float32 [30, 4096], P(None, ('region', 'wave')), may hold values from 1 to 10
- observe: float32 [35, 32768], P(None, ('region', 'wave')), may hold values from 0.1 to 1
- owner: int32 [32768, 1], P(('region', 'wave')), may hold values from 0 to 127; in each aligned block of 256 rows (0 to 255, 256 to 511, ...) at most 4 rows name the same one
- coarse_local: int32 [32768], P(('region', 'wave')), may hold values from 0 to 31
- child: int32 [32768], P(('region', 'wave')), may hold values from 0 to 7
- neighbor: int32 [4, 32768], P(None, ('region', 'wave')), may hold values from 0 to 1151
- orient: int32 [4, 32768], P(None, ('region', 'wave')), may hold values from 0 to 5
- send_face: int32 [16384], P(('region', 'wave')), may hold values from 0 to 1023
Outputs:
- delta_next: float32 [9, 35, 32768], P(None, None, ('region', 'wave'))
- adjoint_next: float32 [9, 35, 32768], P(None, None, ('region', 'wave'))
- hess_vec: float32 [30, 4096], P(None, ('region', 'wave'))
The draws below stay inside these ranges and needn't reach their ends.
Inputs may be any that keep to these rules, and one draw needn't show every extreme that they name: `owner`: no more than 4 fine elements of one device have coarse elements owned by one device, and that number is reached. `send_face`: entries w * 4 to w * 4 + 3 of a device name its traces for wave partition w.
All inputs are finite; a program needn't handle non-finite values.
Results may differ from the reference program's by a relative error of at most 0.0003.
Values sent between devices are 32-bit elements; how exact they have to be, the bound alone decides.
A program may use at most 128 MiB of HBM per device.

```python
import math
import jax
import jax.numpy as jnp
import numpy as np
from jax import lax

FIELDS = 9
NODES = 35
FACE_NODES = 15
PARAMS = 3
PMODES = 10
CHILDREN = 8
E_DEV = 256
CB_DEV = 32
CAP = 4
CAPF = 4
TABLE = 1152
BLOCK = 30
FINE = 32768
COARSE = 4096
SENT = 16384
N_REGION = 4
N_WAVE = 32
DEVICES = 128


def place_ends(values, key, low, largest):
    longest = values.shape.index(max(values.shape))
    spots = []
    for shift in (0, 1):
        where = [jax.random.randint(jax.random.fold_in(key, axis), (), 0, length) for axis, length in enumerate(values.shape)]
        where[longest] = (where[longest] + shift) % values.shape[longest]
        spots.append(tuple(where))
    return values.at[spots[0]].set(low).at[spots[1]].set(largest)


def levels(rng, extent, split, low, top_value):
    loudness, own = 1.0, jax.random.fold_in(rng, 6)
    for axis_at, blocks in split:
        steps = jnp.exp(jax.random.uniform(jax.random.fold_in(own, axis_at), (blocks,), jnp.float32, low / len(split), top_value / len(split)))
        loudness = loudness * jnp.repeat(steps, extent[axis_at] // blocks).reshape([-1 if axis == axis_at else 1 for axis in range(len(extent))])
    return loudness


def routed_block(stream_key, own, number, rows, number_of, top, most, slope):
    order = jax.random.permutation(stream_key, number_of)
    heavy_load, common = load_shares(number_of, rows * top, most, slope, True), load_shares(number_of, rows * top, most, slope, False)
    places = jnp.arange(number_of)

    def named(lengths, turn):
        used = int((lengths > 0).sum())
        fixed = max(1, used // 4)
        shifted = fixed + (places - fixed + turn * (used - fixed)) % max(1, number_of - fixed)
        return jnp.zeros((number_of,), jnp.int32).at[order[jnp.where(places < fixed, places, shifted)]].set(jnp.asarray(lengths, jnp.int32))

    lengths = jnp.where(number % 4 == 0, named(heavy_load, number // 4), named(common, number - number // 4 - 1))
    mixed = jax.random.permutation(jax.random.fold_in(own, 3), number_of)
    donor, sink = mixed[0:number_of // 2 * 2:2], mixed[1:number_of // 2 * 2:2]
    slack = jnp.minimum(lengths[donor] - 1, most - lengths[sink]) // 2
    slack = jnp.where((donor == order[0]) | (sink == order[0]) | (lengths[sink] == 0), 0, jnp.maximum(slack, 0))
    shifted = jax.random.randint(jax.random.fold_in(own, 4), (number_of // 2,), 0, 1 << 20) % (slack + 1)
    lengths = lengths.at[donor].add(-shifted).at[sink].add(shifted)
    labels = jnp.searchsorted(jnp.cumsum(lengths), jnp.arange(rows * top), side="right").astype(jnp.int32)
    table = labels.reshape(top, rows).T
    table = table[jax.random.permutation(jax.random.fold_in(own, 1), rows)]
    turn = jax.random.randint(jax.random.fold_in(own, 2), (rows, 1), 0, top)
    return jnp.take_along_axis(table, (jnp.arange(top)[None, :] + turn) % top, axis=1)


def load_shares(amount, total, bound, slope, full):
    loads = [(1 << 20) // math.isqrt(standing ** slope) + 1 for standing in range(1, amount + 1)]
    largest = bound if full else min(bound, max(-(-total // amount), total * loads[0] // sum(loads)))
    least = 1 if total - largest >= amount - 1 else 0
    given, surplus = [largest] + [least] * (amount - 1), total - largest - least * (amount - 1)
    while surplus > 0:
        free = [i for i in range(1, amount) if given[i] < largest] or [i for i in range(1, amount) if given[i] < bound]
        whole, budget = sum([loads[i] for i in free]), surplus
        for i in free:
            addition = min(bound - given[i], max(1, budget * loads[i] // whole), surplus)
            given[i] = given[i] + addition
            surplus = surplus - addition
    return np.array(given)


def noise(key, dims, spread, bound, split=(), kind=jnp.bfloat16):
    drawn = jax.random.normal(key, dims, jnp.float32) * spread
    if len(split) > 0:
        drawn = levels(key, dims, split, -0.22, 0.18) * drawn
    return jnp.clip(drawn, min=-bound, max=bound).astype(kind)


def setup_inputs(seed: int = 0) -> dict:
    splits = jax.random.split(jax.random.key(seed), 20)
    state0 = noise(splits[0], (FIELDS, NODES, FINE), 1.0, 6.0, ((2, 128),), jnp.float32)
    delta = noise(splits[1], (FIELDS, NODES, FINE), 1.0, 6.0, ((2, 128),), jnp.float32)
    adjoint = noise(splits[2], (FIELDS, NODES, FINE), 1.0, 6.0, ((2, 128),), jnp.float32)
    model = jnp.clip(jnp.exp(math.log(2.0) - 1.3862944 * jax.random.uniform(splits[3], (PARAMS, NODES, FINE), jnp.float32) ** levels(splits[3], (PARAMS, NODES, FINE), ((2, 128),), -0.2, 0.2)), 0.5, 2.0)
    geometry = noise(splits[4], (9, FINE), 0.6, 4.0, ((1, 128),), jnp.float32)
    normals = jnp.clip(jax.random.uniform(splits[5], (3, 4, FINE), jnp.float32, -1.0, 1.0) * levels(splits[5], (3, 4, FINE), ((2, 128),), -0.4, 0.0), -1.0, 1.0)
    face_scale = jnp.clip(jnp.exp(math.log(2.0) - 1.3862944 * jax.random.uniform(splits[6], (4, FINE), jnp.float32) ** levels(splits[6], (4, FINE), ((1, 128),), -0.2, 0.2)), 0.5, 2.0)
    derivative = noise(splits[7], (3, NODES, NODES), NODES ** -0.5, 1.0, (), jnp.float32)
    lift = noise(splits[8], (4, NODES, FACE_NODES), FACE_NODES ** -0.5, 1.5, (), jnp.float32)
    prolong = noise(splits[9], (CHILDREN, NODES, PMODES), PMODES ** -0.5, 2.0, (), jnp.float32)
    coarse_step = noise(splits[10], (BLOCK, COARSE), 1.0, 6.0, ((1, 128),), jnp.float32)
    reg_weight = jnp.clip(jnp.exp(math.log(10.0) - 2.3025851 * jax.random.uniform(splits[11], (BLOCK, COARSE), jnp.float32) ** levels(splits[11], (BLOCK, COARSE), ((1, 128),), -0.2, 0.2)), 1.0, 10.0)
    observe = jnp.clip(jnp.exp(math.log(1.0) - 2.3025851 * jax.random.uniform(splits[12], (NODES, FINE), jnp.float32) ** levels(splits[12], (NODES, FINE), ((1, 128),), -0.2, 0.2)), 0.1, 1.0)
    owner_keys = jax.random.split(jax.random.fold_in(splits[13], 1), FINE // E_DEV)
    owner_turns = jax.random.permutation(jax.random.fold_in(splits[13], 3), FINE // E_DEV)
    owner = jax.vmap(lambda own, number: routed_block(jax.random.fold_in(splits[13], 2), own, number, E_DEV, DEVICES, 1, CAP, 2))(owner_keys, owner_turns).reshape((FINE, 1))
    coarse_local = place_ends(jax.random.randint(splits[14], (FINE,), 0, CB_DEV), jax.random.fold_in(splits[14], 1), 0, CB_DEV - 1).astype(jnp.int32)
    child = place_ends(jax.random.randint(splits[15], (FINE,), 0, CHILDREN), jax.random.fold_in(splits[15], 1), 0, CHILDREN - 1).astype(jnp.int32)
    neighbor = place_ends(jax.random.randint(splits[16], (4, FINE), 0, TABLE), jax.random.fold_in(splits[16], 1), 0, TABLE - 1).astype(jnp.int32)
    orient = place_ends(jax.random.randint(splits[17], (4, FINE), 0, 6), jax.random.fold_in(splits[17], 1), 0, 5).astype(jnp.int32)
    send_face = place_ends(jax.random.randint(splits[18], (SENT,), 0, 4 * E_DEV), jax.random.fold_in(splits[18], 1), 0, (4 * E_DEV) - 1).astype(jnp.int32)
    return dict(state0=state0, delta=delta, adjoint=adjoint, model=model, geometry=geometry, normals=normals, face_scale=face_scale, derivative=derivative, lift=lift, prolong=prolong, coarse_step=coarse_step, reg_weight=reg_weight, observe=observe, owner=owner, coarse_local=coarse_local, child=child, neighbor=neighbor, orient=orient, send_face=send_face)


time_step = 0.2
penalty = 0.5
stress_of = ((0, 5, 4), (5, 1, 3), (4, 3, 2))
voigt_pairs = ((0, 0), (1, 1), (2, 2), (1, 2), (0, 2), (0, 1))
stress_diag = (1.0, 1.0, 1.0, 0.0, 0.0, 0.0)


def tables():
    triangle = [(along_one, along_two) for along_one in range(5) for along_two in range(5 - along_one)]
    volume_nodes = [(along_one, along_two, along_three) for along_one in range(5) for along_two in range(5 - along_one) for along_three in range(5 - along_one - along_two)]
    face_index = np.zeros((15, 4), np.int32)
    for entry_pos, pair_ab in enumerate(triangle):
        places = [(pair_ab[0], pair_ab[1], 0), (pair_ab[0], 0, pair_ab[1]), (0, pair_ab[0], pair_ab[1]), (pair_ab[0], pair_ab[1], 4 - pair_ab[0] - pair_ab[1])]
        for face_id, node_key in enumerate(places):
            face_index[entry_pos, face_id] = volume_nodes.index(node_key)
    orders = [(0, 1, 2), (1, 2, 0), (2, 0, 1), (0, 2, 1), (2, 1, 0), (1, 0, 2)]
    turning = np.zeros((6, 15), np.int32)
    for orient_id, ordering in enumerate(orders):
        for entry_pos, pair_ab in enumerate(triangle):
            coords = (pair_ab[0], pair_ab[1], 4 - pair_ab[0] - pair_ab[1])
            turning[orient_id, entry_pos] = triangle.index((coords[ordering[0]], coords[ordering[1]]))
    return face_index, turning


def pick_traces(field, chosen, face_index):
    elements = field.shape[2]
    face_ids = chosen // elements
    elem_ids = chosen % elements
    return field[:, jnp.asarray(face_index)[:, face_ids], elem_ids[None, :]]


def operator_terms(field, remote, neighbor, orient, geometry, normals, face_scale, derivative, lift, face_index, turning, with_penalty):
    elements = field.shape[2]
    highest = lax.Precision.HIGHEST
    inner = field[:, face_index, :].reshape(9, 15, 4 * elements)
    table = jnp.concatenate([inner, remote], axis=2)
    outer = table[:, :, neighbor.reshape(-1)]
    rotate = jnp.asarray(turning)[orient.reshape(-1)].T
    outer = jnp.take_along_axis(outer, rotate[None, :, :], axis=1)
    jump = (outer - inner).reshape(9, 15, 4, elements)
    local_grad = jnp.einsum("knm,cme->ckne", derivative, field, precision=highest)
    physical = jnp.einsum("ike,ckne->cine", geometry.reshape(3, 3, elements), local_grad, precision=highest)
    half_scale = 0.5 * face_scale[None, :, :]
    channels = []
    for row_id in range(3):
        channels.append(half_scale * sum(normals[col_id][None] * jump[3 + stress_of[row_id][col_id]] for col_id in range(3)))
    channels.append(half_scale * sum(normals[col_id][None] * jump[col_id] for col_id in range(3)))
    for pair_ij in voigt_pairs:
        channels.append(half_scale * (normals[pair_ij[0]][None] * jump[pair_ij[1]] + normals[pair_ij[1]][None] * jump[pair_ij[0]]))
    if with_penalty:
        for comp_id in range(9):
            channels.append(penalty * face_scale[None, :, :] * jump[comp_id])
    lifted = jnp.einsum("fnm,cmfe->cne", lift, jnp.stack(channels), precision=highest)
    terms_b = jnp.stack([sum(physical[3 + stress_of[row_id][col_id], col_id] for col_id in range(3)) + lifted[row_id] for row_id in range(3)])
    terms_lam = sum(physical[col_id, col_id] for col_id in range(3)) + lifted[3]
    terms_mu = jnp.stack([physical[pair_ij[1], pair_ij[0]] + physical[pair_ij[0], pair_ij[1]] + lifted[4 + voigt_id] for voigt_id, pair_ij in enumerate(voigt_pairs)])
    pen_terms = lifted[10:19] if with_penalty else None
    return terms_b, terms_lam, terms_mu, pen_terms


def apply_model(params, terms_b, terms_lam, terms_mu):
    velocity = params[0][None] * terms_b
    diagonal = jnp.asarray(stress_diag, jnp.float32)[:, None, None]
    stress = params[2][None] * terms_mu + diagonal * (params[1] * terms_lam)[None]
    return jnp.concatenate([velocity, stress], axis=0)


def section(state0, delta, adjoint, model, geometry, normals, face_scale, observe, neighbor, orient, remote_state, remote_delta, remote_adjoint, fetched, child, derivative, lift, prolong, face_index, turning):
    elements = state0.shape[2]
    highest = lax.Precision.HIGHEST
    shapes = prolong[child]
    step_fine = jnp.einsum("enk,pke->pne", shapes, fetched.reshape(3, -1, elements), precision=highest)
    base = operator_terms(state0, remote_state, neighbor, orient, geometry, normals, face_scale, derivative, lift, face_index, turning, False)
    moved = operator_terms(delta, remote_delta, neighbor, orient, geometry, normals, face_scale, derivative, lift, face_index, turning, True)
    backed = operator_terms(adjoint, remote_adjoint, neighbor, orient, geometry, normals, face_scale, derivative, lift, face_index, turning, True)
    delta_next = delta + time_step * (apply_model(model, moved[0], moved[1], moved[2]) + moved[3] + apply_model(step_fine, base[0], base[1], base[2]))
    adjoint_next = adjoint + time_step * (apply_model(model, backed[0], backed[1], backed[2]) + backed[3] + observe[None] * delta_next)
    grad_b = time_step * jnp.sum(adjoint_next[0:3] * base[0], axis=0)
    grad_lam = time_step * jnp.sum(adjoint_next[3:6], axis=0) * base[1]
    grad_mu = time_step * jnp.sum(adjoint_next[3:9] * base[2], axis=0)
    fine_grad = jnp.stack([grad_b, grad_lam, grad_mu])
    restricted = jnp.einsum("enk,pne->pke", shapes, fine_grad, precision=highest).reshape(-1, elements)
    return delta_next, adjoint_next, restricted


def reference(state0, delta, adjoint, model, geometry, normals, face_scale, derivative, lift, prolong, coarse_step, reg_weight, observe, owner, coarse_local, child, neighbor, orient, send_face):
    face_index, turning = tables()

    def per_device(array):
        return jnp.moveaxis(array.reshape(array.shape[:-1] + (DEVICES, E_DEV)), -2, 0)

    def to_whole(array):
        moved = jnp.moveaxis(array, 0, -2)
        return moved.reshape(moved.shape[:-2] + (FINE,))

    chosen = send_face.reshape(DEVICES, N_WAVE * CAPF)

    def received(field):
        sent = jax.vmap(lambda one_field, one_list: pick_traces(one_field, one_list, face_index))(per_device(field), chosen)
        sent = sent.reshape(N_REGION, N_WAVE, 9, 15, N_WAVE, CAPF)
        return jnp.transpose(sent, (0, 4, 2, 3, 1, 5)).reshape(DEVICES, 9, 15, N_WAVE * CAPF)

    global_ids = (owner[:, 0] * CB_DEV + coarse_local).astype(jnp.int32)
    fetched = coarse_step[:, global_ids]
    inputs = (per_device(state0), per_device(delta), per_device(adjoint), per_device(model), per_device(geometry), per_device(normals), per_device(face_scale), per_device(observe), per_device(neighbor), per_device(orient), received(state0), received(delta), received(adjoint), per_device(fetched), per_device(child))

    def run_one(pack):
        return section(pack[0], pack[1], pack[2], pack[3], pack[4], pack[5], pack[6], pack[7], pack[8], pack[9], pack[10], pack[11], pack[12], pack[13], pack[14], derivative, lift, prolong, face_index, turning)

    delta_dev, adjoint_dev, restricted_dev = lax.map(run_one, inputs)
    restricted = to_whole(restricted_dev)
    summed = jax.ops.segment_sum(restricted.T, global_ids, num_segments=COARSE).T
    hess_vec = summed + reg_weight * coarse_step
    return to_whole(delta_dev), to_whole(adjoint_dev), hess_vec
```

```python
import functools

import jax
import jax.numpy as jnp
import numpy as np
from jax import lax
from jax.experimental import pallas as pl
from jax.experimental.pallas import tpu as pltpu
from jax.sharding import PartitionSpec as P

f32, bf16, i32, i16 = jnp.float32, jnp.bfloat16, jnp.int32, jnp.int16
MESH = pl.DeviceIdType.MESH

STEP = 0.2
STRESS = ((0, 5, 4), (5, 1, 3), (4, 3, 2))
OFF = ((1, 2), (0, 2), (0, 1))
NF, NN, E, NW, ND = 9, 35, 256, 32, 128
OWN, TAB = 1024, 1152
ROWS = 27 * 16


def tables():
    triangle = [(a, b) for a in range(5) for b in range(5 - a)]
    nodes = [(a, b, c) for a in range(5) for b in range(5 - a) for c in range(5 - a - b)]
    face = np.zeros((4, 15), np.int32)
    for at, (a, b) in enumerate(triangle):
        for f, key in enumerate(((a, b, 0), (a, 0, b), (0, a, b), (a, b, 4 - a - b))):
            face[f, at] = nodes.index(key)
    orders = [(0, 1, 2), (1, 2, 0), (2, 0, 1), (0, 2, 1), (2, 1, 0), (1, 0, 2)]
    turning = np.zeros((6, 15), np.int32)
    for o, order in enumerate(orders):
        for at, (a, b) in enumerate(triangle):
            triple = (a, b, 4 - a - b)
            turning[o, at] = triangle.index((triple[order[0]], triple[order[1]]))
    return face, turning


def constants():
    face, turning = tables()
    pick = np.zeros((128, 144), np.float32)
    for f in range(4):
        for m in range(15):
            pick[f * 16 + m, face[f, m]] = 1.0
            pick[64 + f * 16 + m, 48 + face[f, m]] = 1.0
    turn = np.full((16, 128), 15, np.int32)
    for o in range(6):
        turn[:15, o] = turning[o]
    return pick, turn


def split(x):
    hi = x.astype(bf16)
    lo = (x - hi.astype(f32)).astype(bf16)
    return hi, lo


def nn(a, b):
    return lax.dot_general(a, b, (((1,), (0,)), ((), ())), preferred_element_type=f32)


def nt(a, b):
    return lax.dot_general(a, b, (((1,), (1,)), ((), ())), preferred_element_type=f32)


def tn(a, b):
    return lax.dot_general(a, b, (((0,), (0,)), ((), ())), preferred_element_type=f32)


def iota(shape, dim, kind=i32):
    return lax.broadcasted_iota(kind, shape, dim)


def below(x, rows):
    return jnp.concatenate([x, jnp.zeros((rows - x.shape[0], x.shape[1]), x.dtype)], axis=0)


def lanes3(x, width):
    hi = x.astype(bf16).astype(f32)
    lo = x - hi
    zero = jnp.zeros((x.shape[0], width - x.shape[1]), f32)
    return jnp.concatenate([hi, zero, hi, zero, lo, zero], axis=1).astype(bf16)


def rows3(x):
    hi, lo = split(x)
    return jnp.concatenate([hi, lo, hi], axis=0)


def kernel(
    s0, dl, ad, model, geometry, normals, face_scale, derivative, lift, prolong, coarse, reg, observe,
    owner, local, child, neighbor, orient, send_face, pick, turn,
    out_d, out_a, out_h,
    tab, hot, dq, jump, hn, xl, fs, ltr, rst, c1,
    tr_s, tr_r, rq_s, rq_r, an_s, an_r, pt_s, pt_r,
    ssem, rsem,
):
    region, wave = lax.axis_index("region"), lax.axis_index("wave")
    me = region * NW + wave
    barrier = pltpu.get_barrier_semaphore()

    def where_is(i):
        d = lax.rem(me + i, ND)
        return d, (lax.div(d, NW), lax.rem(d, NW))

    def greet(i, c):
        pl.semaphore_signal(barrier, inc=1, device_id=where_is(i)[1], device_id_type=MESH)
        return c

    lax.fori_loop(1, ND, greet, 0)

    def send_rows(src, dst, at):
        def one(i, c):
            d, there = where_is(i)
            pltpu.make_async_remote_copy(
                src_ref=src.at[d], dst_ref=dst.at[me], send_sem=ssem.at[at], recv_sem=rsem.at[at],
                device_id=there, device_id_type=MESH,
            ).start()
            return c

        lax.fori_loop(1, ND, one, 0)
        dst[pl.ds(me, 1)] = src[pl.ds(me, 1)]

    def wait_rows(ref, sem):
        part = ref.at[pl.ds(0, ND - 1)]
        pltpu.make_async_copy(part, part, sem).wait()

    u = (iota((ND, E), 0) == owner[...]).astype(f32).astype(bf16)
    ub = u.astype(f32)
    tri = (iota((E, E), 0) < iota((E, E), 1)).astype(f32).astype(bf16)
    before = jnp.sum(nn(u, tri) * ub, axis=0, keepdims=True).astype(i32)
    code = before * 32 + local[...]
    vt = (iota((128, E), 0) == code).astype(f32).astype(bf16)
    rq_s.reshape(ND, 128)[...] = nt(u, vt)

    for k in range(3):
        c1[k * 40:(k + 1) * 40, :] = lanes3(below(derivative[k], 40), 48)
    c1[120:248, :] = pick[...]
    for s, ref in enumerate((s0, dl, ad)):
        for c in range(NF):
            sc = s * NF + c
            got = nn(c1[...], rows3(below(ref[c], 48)))
            dq[sc] = got[0:120]
            for f in range(4):
                span = slice(f * E, (f + 1) * E)
                tab[0, sc * 16:(sc + 1) * 16, span] = got[120 + f * 16:136 + f * 16].astype(bf16)
                tab[1, sc * 16:(sc + 1) * 16, span] = got[184 + f * 16:200 + f * 16].astype(bf16)

    pickt = (iota((OWN, 128), 0) == send_face[...]).astype(f32).astype(bf16)
    sent = nn(tab[0, :, 0:OWN], pickt) + nn(tab[1, :, 0:OWN], pickt)
    sent = below(sent, 512)
    for j in range(4):
        tr_s.reshape(4, 128, 128)[j] = sent[j * 128:(j + 1) * 128].T

    pl.semaphore_wait(barrier, ND - 1)
    send_rows(rq_s, rq_r, 0)

    def send_trace(i, c):
        w = lax.rem(wave + i, NW)
        pltpu.make_async_remote_copy(
            src_ref=tr_s.at[:, pl.ds(w, 1)], dst_ref=tr_r.at[:, pl.ds(wave, 1)],
            send_sem=ssem.at[1], recv_sem=rsem.at[1], device_id=(region, w), device_id_type=MESH,
        ).start()
        return c

    lax.fori_loop(1, NW, send_trace, 0)
    tr_r[:, pl.ds(wave, 1)] = tr_s[:, pl.ds(wave, 1)]

    for f in range(4):
        row = neighbor[f:f + 1, :].astype(i16)
        hot[:, f * E:(f + 1) * E] = jnp.where(
            iota((TAB, E), 0, i16) == row, jnp.ones((), bf16), jnp.zeros((), bf16)
        )

    wait_rows(rq_r, rsem.at[0])
    asked = rq_r.reshape(ND, 128)[...].astype(bf16)
    cs = jnp.concatenate([coarse[...], jnp.zeros((2, 32), f32)], axis=0)
    cs4 = jnp.concatenate([cs] * 4, axis=1)
    cs16 = jnp.concatenate([cs4] * 4, axis=0)
    same = lax.div(iota((128, 128), 0), 32) == lax.div(iota((128, 128), 1), 32)
    bh, bl = split(jnp.where(same, cs16, 0.0))
    an_s.reshape(ND, 128)[...] = nt(asked, bh) + nt(asked, bl)
    send_rows(an_s, an_r, 2)

    for f in range(4):
        span = slice(f * E, (f + 1) * E)
        jump[:, span] = nn(tab[0, :, 0:OWN], hot[0:OWN, span]) + nn(tab[1, :, 0:OWN], hot[0:OWN, span])

    part = tr_r.at[:, pl.ds(0, NW - 1)]
    pltpu.make_async_copy(part, part, rsem.at[1]).wait()
    for j in range(4):
        rows = min(128, ROWS - j * 128)
        hi, lo = split(tr_r.reshape(4, 128, 128)[j].T[0:rows])
        tab[0, j * 128:j * 128 + rows, OWN:TAB] = hi
        tab[1, j * 128:j * 128 + rows, OWN:TAB] = lo
    for f in range(4):
        span = slice(f * E, (f + 1) * E)
        jump[:, span] += nn(tab[0, :, OWN:TAB], hot[OWN:TAB, span]) + nn(tab[1, :, OWN:TAB], hot[OWN:TAB, span])

    for f in range(4):
        span = slice(f * E, (f + 1) * E)
        h = 0.5 * face_scale[f:f + 1, :]
        for j in range(3):
            hn[j, :, span] = jnp.broadcast_to(h * normals[j, f:f + 1, :], (8, E))
        hn[3, :, span] = jnp.broadcast_to(h, (8, E))

    ltr[...] = jnp.zeros_like(ltr)
    for f in range(4):
        for m in range(15):
            ltr[f * 16 + m:f * 16 + m + 1, 0:NN] = lift[m, f:f + 1, :]
    lh, ll = split(ltr[...].T[0:40])
    lmat = jnp.concatenate([lh.astype(f32), lh.astype(f32), ll.astype(f32)], axis=1).astype(bf16)

    for f in range(4):
        span = slice(f * E, (f + 1) * E)
        o = orient[f:f + 1, :]
        idx = jnp.full((16, E), 15, i32)
        for q in range(6):
            idx = jnp.where(o == q, turn[:, q:q + 1], idx)
        low = idx < 8
        idx = idx & 7
        ia, ib = idx[0:8], idx[8:16]
        for sc in range(27):
            a = jump[sc * 16:sc * 16 + 8, span]
            b = jump[sc * 16 + 8:sc * 16 + 16, span]
            own = tab[0, sc * 16:sc * 16 + 16, span].astype(f32) + tab[1, sc * 16:sc * 16 + 16, span].astype(f32)
            for t, ix in enumerate((ia, ib)):
                ga = jnp.take_along_axis(a, ix, axis=0, mode="promise_in_bounds")
                gb = jnp.take_along_axis(b, ix, axis=0, mode="promise_in_bounds")
                jump[sc * 16 + t * 8:sc * 16 + t * 8 + 8, span] = (
                    jnp.where(low[t * 8:t * 8 + 8], ga, gb) - own[t * 8:t * 8 + 8]
                )

    geo = [geometry[q:q + 1, :] for q in range(9)]

    def grad(sc, i):
        return sum(geo[3 * i + k] * dq[sc, k * 40:(k + 1) * 40, :] for k in range(3))

    for s in range(3):
        for f in range(4):
            span = slice(f * E, (f + 1) * E)
            n = [jnp.concatenate([hn[j, :, span]] * 2, axis=0) for j in range(4)]
            q = [jump[(s * NF + c) * 16:(s * NF + c) * 16 + 16, span] for c in range(NF)]
            chans = [sum(n[j] * q[3 + STRESS[i][j]] for j in range(3)) for i in range(3)]
            chans += [n[j] * q[j] for j in range(3)]
            chans += [n[i] * q[j] + n[j] * q[i] for i, j in OFF]
            if s > 0:
                chans += [n[3] * q[c] for c in range(NF)]
            for at, g in enumerate(chans):
                hi, lo = split(g)
                xl[at, f * 16:f * 16 + 16, :] = hi
                xl[at, 64 + f * 16:80 + f * 16, :] = lo
                xl[at, 128 + f * 16:144 + f * 16, :] = hi
        base = s * NF
        for i in range(3):
            fs[s, i] = nn(lmat, xl[i]) + sum(grad(base + 3 + STRESS[i][j], j) for j in range(3))
            fs[s, 3 + i] = nn(lmat, xl[3 + i]) + grad(base + i, i)
        for at, (i, j) in enumerate(OFF):
            fs[s, 6 + at] = nn(lmat, xl[6 + at]) + grad(base + j, i) + grad(base + i, j)
        if s > 0:
            for c in range(NF):
                fs[s, 9 + c] = nn(lmat, xl[9 + c])

    wait_rows(an_r, rsem.at[2])
    ah, al = split(an_r.reshape(ND, 128)[...])
    slot = lax.div(iota((128, E), 0), 32) == before
    found = jnp.where(slot, tn(ah, u) + tn(al, u), 0.0)
    found = found[0:32] + found[32:64] + found[64:96] + found[96:128]
    mask = (iota((8, E), 0) == child[...]).astype(f32)
    pm = prolong[...].reshape(80, NN)
    pm40 = jnp.concatenate([pm, jnp.zeros((80, 5), f32)], axis=1)
    ph, pw = split(pm40)
    pm3 = jnp.concatenate([ph, ph, pw], axis=0)
    fine = []
    for p in range(3):
        z = jnp.concatenate([mask * found[p * 10 + k:p * 10 + k + 1, :] for k in range(10)], axis=0)
        fine.append(tn(pm3, rows3(z)))

    m0, m1, m2 = (below(model[p], 40) for p in range(3))

    def lam(s):
        return fs[s, 3] + fs[s, 4] + fs[s, 5]

    def mu(s, k):
        return 2.0 * fs[s, 3 + k] if k < 3 else fs[s, 3 + k]

    lam0 = lam(0)
    lam1 = m1 * lam(1) + fine[1] * lam0
    lam2 = m1 * lam(2)
    obs = below(observe[...], 40)
    gb = jnp.zeros((40, E), f32)
    tr = jnp.zeros((40, E), f32)
    gm = jnp.zeros((40, E), f32)
    for c in range(NF):
        if c < 3:
            wave_d = m0 * fs[1, c] + fine[0] * fs[0, c]
            wave_a = m0 * fs[2, c]
        else:
            wave_d = m2 * mu(1, c - 3) + fine[2] * mu(0, c - 3)
            wave_a = m2 * mu(2, c - 3)
            if c < 6:
                wave_d = wave_d + lam1
                wave_a = wave_a + lam2
        nd = below(dl[c], 40) + STEP * (wave_d + fs[1, 9 + c])
        na = below(ad[c], 40) + STEP * (wave_a + fs[2, 9 + c] + obs * nd)
        out_d[c] = nd[0:NN]
        out_a[c] = na[0:NN]
        if c < 3:
            gb = gb + na * fs[0, c]
        else:
            gm = gm + na * mu(0, c - 3)
            if c < 6:
                tr = tr + na
    fine_grad = (STEP * gb, STEP * tr * lam0, STEP * gm)

    pm144 = lanes3(pm, 48)
    rst[...] = jnp.zeros_like(rst)
    for p in range(3):
        r = nn(pm144, rows3(below(fine_grad[p], 48)))
        rst[p * 10:(p + 1) * 10, :] = jnp.sum(r.reshape(10, 8, E) * mask[None], axis=1)
    wh, wl = split(jnp.where(slot, jnp.concatenate([rst[...]] * 4, axis=0), 0.0))
    pt_s.reshape(ND, 128)[...] = nt(u, wh) + nt(u, wl)
    send_rows(pt_s, pt_r, 3)
    wait_rows(pt_r, rsem.at[3])
    gh, gl = split(pt_r.reshape(ND, 128)[...])
    total = jnp.where(same, tn(gh, asked) + tn(gl, asked), 0.0)
    total = total[0:32] + total[32:64] + total[64:96] + total[96:128]
    total = total[:, 0:32] + total[:, 32:64] + total[:, 64:96] + total[:, 96:128]
    out_h[...] = total[0:30] + reg[...] * coarse[...]

    wait_rows(rq_s, ssem.at[0])
    part = tr_s.at[:, pl.ds(0, NW - 1)]
    pltpu.make_async_copy(part, part, ssem.at[1]).wait()
    wait_rows(an_s, ssem.at[2])
    wait_rows(pt_s, ssem.at[3])


def body(
    state0, delta, adjoint, model, geometry, normals, face_scale, derivative, lift, prolong, coarse_step, reg_weight,
    observe, owner, coarse_local, child, neighbor, orient, send_face,
):
    pick, turn = constants()
    ops = (
        state0, delta, adjoint, model, geometry, normals, face_scale, derivative,
        lift.transpose(2, 0, 1), prolong.transpose(2, 0, 1), coarse_step, reg_weight, observe,
        owner.reshape(1, E), coarse_local.reshape(1, E), child.reshape(1, E), neighbor, orient, send_face.reshape(1, 128),
        jnp.asarray(pick, bf16), jnp.asarray(turn),
    )
    vmem = pl.BlockSpec(memory_space=pltpu.VMEM)
    row = pltpu.VMEM((ND, 1, 128), f32)
    return pl.pallas_call(
        kernel,
        out_shape=(
            jax.ShapeDtypeStruct((NF, NN, E), f32),
            jax.ShapeDtypeStruct((NF, NN, E), f32),
            jax.ShapeDtypeStruct((30, 32), f32),
        ),
        in_specs=[vmem] * len(ops),
        out_specs=(vmem, vmem, vmem),
        scratch_shapes=[
            pltpu.VMEM((2, ROWS, TAB), bf16),
            pltpu.VMEM((TAB, OWN), bf16),
            pltpu.VMEM((27, 120, E), f32),
            pltpu.VMEM((ROWS, OWN), f32),
            pltpu.VMEM((4, 8, OWN), f32),
            pltpu.VMEM((18, 192, E), bf16),
            pltpu.VMEM((3, 18, 40, E), f32),
            pltpu.VMEM((64, 128), f32),
            pltpu.VMEM((32, E), f32),
            pltpu.VMEM((248, 144), bf16),
            pltpu.VMEM((4, NW, 4, 128), f32),
            pltpu.VMEM((4, NW, 4, 128), f32),
            row, row, row, row, row, row,
            pltpu.SemaphoreType.DMA((4,)),
            pltpu.SemaphoreType.DMA((4,)),
        ],
        compiler_params=pltpu.CompilerParams(
            collective_id=0, has_side_effects=True, vmem_limit_bytes=48 * 1024 * 1024
        ),
    )(*ops)


def solution(mesh):
    both = ("region", "wave")
    placed = (
        P(None, None, both), P(None, None, both), P(None, None, both), P(None, None, both), P(None, both),
        P(None, None, both), P(None, both), P(), P(), P(), P(None, both), P(None, both), P(None, both),
        P(both, None), P(both), P(both), P(None, both), P(None, both), P(both),
    )
    return jax.shard_map(
        body, mesh=mesh, in_specs=placed,
        out_specs=(P(None, None, both), P(None, None, both), P(None, both)), check_vma=False,
    )
```

```python
import functools

import jax
import jax.numpy as jnp
import numpy as np
from jax import lax
from jax.experimental import pallas as pl
from jax.experimental.pallas import tpu as pltpu
from jax.sharding import PartitionSpec as P

f32, bf16, i32, i16 = jnp.float32, jnp.bfloat16, jnp.int32, jnp.int16
MESH = pl.DeviceIdType.MESH

STEP = 0.2
STRESS = ((0, 5, 4), (5, 1, 3), (4, 3, 2))
OFF = ((1, 2), (0, 2), (0, 1))
NF, NN, E, NW, ND = 9, 35, 256, 32, 128
OWN, TAB = 1024, 1152
ROWS = 27 * 16


def tables():
    triangle = [(a, b) for a in range(5) for b in range(5 - a)]
    nodes = [(a, b, c) for a in range(5) for b in range(5 - a) for c in range(5 - a - b)]
    face = np.zeros((4, 15), np.int32)
    for at, (a, b) in enumerate(triangle):
        for f, key in enumerate(((a, b, 0), (a, 0, b), (0, a, b), (a, b, 4 - a - b))):
            face[f, at] = nodes.index(key)
    orders = [(0, 1, 2), (1, 2, 0), (2, 0, 1), (0, 2, 1), (2, 1, 0), (1, 0, 2)]
    turning = np.zeros((6, 15), np.int32)
    for o, order in enumerate(orders):
        for at, (a, b) in enumerate(triangle):
            triple = (a, b, 4 - a - b)
            turning[o, at] = triangle.index((triple[order[0]], triple[order[1]]))
    return face, turning


def constants():
    face, turning = tables()
    pick = np.zeros((128, 144), np.float32)
    for f in range(4):
        for m in range(15):
            pick[f * 16 + m, face[f, m]] = 1.0
            pick[64 + f * 16 + m, 48 + face[f, m]] = 1.0
    turn = np.full((16, 128), 15, np.int32)
    for o in range(6):
        turn[:15, o] = turning[o]
    return pick, turn


def split(x):
    hi = x.astype(bf16)
    lo = (x - hi.astype(f32)).astype(bf16)
    return hi, lo


def nn(a, b):
    return lax.dot_general(a, b, (((1,), (0,)), ((), ())), preferred_element_type=f32)


def nt(a, b):
    return lax.dot_general(a, b, (((1,), (1,)), ((), ())), preferred_element_type=f32)


def tn(a, b):
    return lax.dot_general(a, b, (((0,), (0,)), ((), ())), preferred_element_type=f32)


def iota(shape, dim, kind=i32):
    return lax.broadcasted_iota(kind, shape, dim)


def below(x, rows):
    return jnp.concatenate([x, jnp.zeros((rows - x.shape[0], x.shape[1]), x.dtype)], axis=0)


def lanes3(x, width):
    hi = x.astype(bf16).astype(f32)
    lo = x - hi
    zero = jnp.zeros((x.shape[0], width - x.shape[1]), f32)
    return jnp.concatenate([hi, zero, hi, zero, lo, zero], axis=1).astype(bf16)


def rows3(x):
    hi, lo = split(x)
    return jnp.concatenate([hi, lo, hi], axis=0)


N_OPS = 21


def kernel(*refs):
    sources, (out_d, out_a, out_h) = refs[:N_OPS], refs[N_OPS:N_OPS + 3]
    held = refs[N_OPS + 3:2 * N_OPS + 3]
    isem = refs[-1]
    loads = [pltpu.make_async_copy(a, b, isem.at[at]) for at, (a, b) in enumerate(zip(sources, held))]
    for load in loads:
        load.start()
    work(loads, *held, out_d, out_a, out_h, *refs[2 * N_OPS + 3:-1])


def work(
    loads,
    s0, dl, ad, model, geometry, normals, face_scale, derivative, lift, prolong, coarse, reg, observe,
    owner, local, child, neighbor, orient, send_face, pick, turn,
    out_d, out_a, out_h,
    tab, hot, dq, jump, hn, xl, fs, ltr, rst, c1,
    tr_s, tr_r, rq_s, rq_r, an_s, an_r, pt_s, pt_r,
    ssem, rsem,
):
    region, wave = lax.axis_index("region"), lax.axis_index("wave")
    me = region * NW + wave
    barrier = pltpu.get_barrier_semaphore()

    def where_is(i):
        d = lax.rem(me + i, ND)
        return d, (lax.div(d, NW), lax.rem(d, NW))

    def greet(i, c):
        pl.semaphore_signal(barrier, inc=1, device_id=where_is(i)[1], device_id_type=MESH)
        return c

    lax.fori_loop(1, ND, greet, 0)

    def send_rows(src, dst, at):
        def one(i, c):
            d, there = where_is(i)
            pltpu.make_async_remote_copy(
                src_ref=src.at[d], dst_ref=dst.at[me], send_sem=ssem.at[at], recv_sem=rsem.at[at],
                device_id=there, device_id_type=MESH,
            ).start()
            return c

        lax.fori_loop(1, ND, one, 0)
        dst[pl.ds(me, 1)] = src[pl.ds(me, 1)]

    def wait_rows(ref, sem):
        part = ref.at[pl.ds(0, ND - 1)]
        pltpu.make_async_copy(part, part, sem).wait()

    for load in loads:
        load.wait()

    u = (iota((ND, E), 0) == owner[...]).astype(f32).astype(bf16)
    ub = u.astype(f32)
    tri = (iota((E, E), 0) < iota((E, E), 1)).astype(f32).astype(bf16)
    before = jnp.sum(nn(u, tri) * ub, axis=0, keepdims=True).astype(i32)
    code = before * 32 + local[...]
    vt = (iota((128, E), 0) == code).astype(f32).astype(bf16)
    rq_s.reshape(ND, 128)[...] = nt(u, vt)

    for k in range(3):
        c1[k * 40:(k + 1) * 40, :] = lanes3(below(derivative[k], 40), 48)
    c1[120:248, :] = pick[...]
    for s, ref in enumerate((s0, dl, ad)):
        for c in range(NF):
            sc = s * NF + c
            got = nn(c1[...], rows3(below(ref[c], 48)))
            dq[sc] = got[0:120]
            for f in range(4):
                span = slice(f * E, (f + 1) * E)
                tab[0, sc * 16:(sc + 1) * 16, span] = got[120 + f * 16:136 + f * 16].astype(bf16)
                tab[1, sc * 16:(sc + 1) * 16, span] = got[184 + f * 16:200 + f * 16].astype(bf16)

    pickt = (iota((OWN, 128), 0) == send_face[...]).astype(f32).astype(bf16)
    sent = nn(tab[0, :, 0:OWN], pickt) + nn(tab[1, :, 0:OWN], pickt)
    sent = below(sent, 512)
    for j in range(4):
        tr_s.reshape(4, 128, 128)[j] = sent[j * 128:(j + 1) * 128].T

    pl.semaphore_wait(barrier, ND - 1)
    send_rows(rq_s, rq_r, 0)

    def send_trace(i, c):
        w = lax.rem(wave + i, NW)
        pltpu.make_async_remote_copy(
            src_ref=tr_s.at[:, pl.ds(w, 1)], dst_ref=tr_r.at[:, pl.ds(wave, 1)],
            send_sem=ssem.at[1], recv_sem=rsem.at[1], device_id=(region, w), device_id_type=MESH,
        ).start()
        return c

    lax.fori_loop(1, NW, send_trace, 0)
    tr_r[:, pl.ds(wave, 1)] = tr_s[:, pl.ds(wave, 1)]

    for f in range(4):
        row = neighbor[f:f + 1, :].astype(i16)
        hot[:, f * E:(f + 1) * E] = jnp.where(
            iota((TAB, E), 0, i16) == row, jnp.ones((), bf16), jnp.zeros((), bf16)
        )

    wait_rows(rq_r, rsem.at[0])
    asked = rq_r.reshape(ND, 128)[...].astype(bf16)
    cs = jnp.concatenate([coarse[...], jnp.zeros((2, 32), f32)], axis=0)
    cs4 = jnp.concatenate([cs] * 4, axis=1)
    cs16 = jnp.concatenate([cs4] * 4, axis=0)
    same = lax.div(iota((128, 128), 0), 32) == lax.div(iota((128, 128), 1), 32)
    bh, bl = split(jnp.where(same, cs16, 0.0))
    an_s.reshape(ND, 128)[...] = nt(asked, bh) + nt(asked, bl)
    send_rows(an_s, an_r, 2)

    for f in range(4):
        span = slice(f * E, (f + 1) * E)
        jump[:, span] = nn(tab[0, :, 0:OWN], hot[0:OWN, span]) + nn(tab[1, :, 0:OWN], hot[0:OWN, span])

    part = tr_r.at[:, pl.ds(0, NW - 1)]
    pltpu.make_async_copy(part, part, rsem.at[1]).wait()
    for j in range(4):
        rows = min(128, ROWS - j * 128)
        hi, lo = split(tr_r.reshape(4, 128, 128)[j].T[0:rows])
        tab[0, j * 128:j * 128 + rows, OWN:TAB] = hi
        tab[1, j * 128:j * 128 + rows, OWN:TAB] = lo
    for f in range(4):
        span = slice(f * E, (f + 1) * E)
        jump[:, span] += nn(tab[0, :, OWN:TAB], hot[OWN:TAB, span]) + nn(tab[1, :, OWN:TAB], hot[OWN:TAB, span])

    for f in range(4):
        span = slice(f * E, (f + 1) * E)
        h = 0.5 * face_scale[f:f + 1, :]
        for j in range(3):
            hn[j, :, span] = jnp.broadcast_to(h * normals[j, f:f + 1, :], (8, E))
        hn[3, :, span] = jnp.broadcast_to(h, (8, E))

    ltr[...] = jnp.zeros_like(ltr)
    for f in range(4):
        for m in range(15):
            ltr[f * 16 + m:f * 16 + m + 1, 0:NN] = lift[m, f:f + 1, :]
    lh, ll = split(ltr[...].T[0:40])
    lmat = jnp.concatenate([lh.astype(f32), lh.astype(f32), ll.astype(f32)], axis=1).astype(bf16)

    for f in range(4):
        span = slice(f * E, (f + 1) * E)
        o = orient[f:f + 1, :]
        idx = jnp.full((16, E), 15, i32)
        for q in range(6):
            idx = jnp.where(o == q, turn[:, q:q + 1], idx)
        low = idx < 8
        idx = idx & 7
        ia, ib = idx[0:8], idx[8:16]
        for sc in range(27):
            a = jump[sc * 16:sc * 16 + 8, span]
            b = jump[sc * 16 + 8:sc * 16 + 16, span]
            own = tab[0, sc * 16:sc * 16 + 16, span].astype(f32) + tab[1, sc * 16:sc * 16 + 16, span].astype(f32)
            for t, ix in enumerate((ia, ib)):
                ga = jnp.take_along_axis(a, ix, axis=0, mode="promise_in_bounds")
                gb = jnp.take_along_axis(b, ix, axis=0, mode="promise_in_bounds")
                jump[sc * 16 + t * 8:sc * 16 + t * 8 + 8, span] = (
                    jnp.where(low[t * 8:t * 8 + 8], ga, gb) - own[t * 8:t * 8 + 8]
                )

    geo = [geometry[q:q + 1, :] for q in range(9)]

    def grad(sc, i):
        return sum(geo[3 * i + k] * dq[sc, k * 40:(k + 1) * 40, :] for k in range(3))

    for s in range(3):
        for f in range(4):
            span = slice(f * E, (f + 1) * E)
            n = [jnp.concatenate([hn[j, :, span]] * 2, axis=0) for j in range(4)]
            q = [jump[(s * NF + c) * 16:(s * NF + c) * 16 + 16, span] for c in range(NF)]
            chans = [sum(n[j] * q[3 + STRESS[i][j]] for j in range(3)) for i in range(3)]
            chans += [n[j] * q[j] for j in range(3)]
            chans += [n[i] * q[j] + n[j] * q[i] for i, j in OFF]
            if s > 0:
                chans += [n[3] * q[c] for c in range(NF)]
            for at, g in enumerate(chans):
                hi, lo = split(g)
                xl[at, f * 16:f * 16 + 16, :] = hi
                xl[at, 64 + f * 16:80 + f * 16, :] = lo
                xl[at, 128 + f * 16:144 + f * 16, :] = hi
        base = s * NF
        for i in range(3):
            fs[s, i] = nn(lmat, xl[i]) + sum(grad(base + 3 + STRESS[i][j], j) for j in range(3))
            fs[s, 3 + i] = nn(lmat, xl[3 + i]) + grad(base + i, i)
        for at, (i, j) in enumerate(OFF):
            fs[s, 6 + at] = nn(lmat, xl[6 + at]) + grad(base + j, i) + grad(base + i, j)
        if s > 0:
            for c in range(NF):
                fs[s, 9 + c] = nn(lmat, xl[9 + c])

    wait_rows(an_r, rsem.at[2])
    ah, al = split(an_r.reshape(ND, 128)[...])
    slot = lax.div(iota((128, E), 0), 32) == before
    found = jnp.where(slot, tn(ah, u) + tn(al, u), 0.0)
    found = found[0:32] + found[32:64] + found[64:96] + found[96:128]
    mask = (iota((8, E), 0) == child[...]).astype(f32)
    pm = prolong[...].reshape(80, NN)
    pm40 = jnp.concatenate([pm, jnp.zeros((80, 5), f32)], axis=1)
    ph, pw = split(pm40)
    pm3 = jnp.concatenate([ph, ph, pw], axis=0)
    fine = []
    for p in range(3):
        z = jnp.concatenate([mask * found[p * 10 + k:p * 10 + k + 1, :] for k in range(10)], axis=0)
        fine.append(tn(pm3, rows3(z)))

    m0, m1, m2 = (below(model[p], 40) for p in range(3))

    def lam(s):
        return fs[s, 3] + fs[s, 4] + fs[s, 5]

    def mu(s, k):
        return 2.0 * fs[s, 3 + k] if k < 3 else fs[s, 3 + k]

    lam0 = lam(0)
    lam1 = m1 * lam(1) + fine[1] * lam0
    lam2 = m1 * lam(2)
    obs = below(observe[...], 40)
    gb = jnp.zeros((40, E), f32)
    tr = jnp.zeros((40, E), f32)
    gm = jnp.zeros((40, E), f32)
    for c in range(NF):
        if c < 3:
            wave_d = m0 * fs[1, c] + fine[0] * fs[0, c]
            wave_a = m0 * fs[2, c]
        else:
            wave_d = m2 * mu(1, c - 3) + fine[2] * mu(0, c - 3)
            wave_a = m2 * mu(2, c - 3)
            if c < 6:
                wave_d = wave_d + lam1
                wave_a = wave_a + lam2
        nd = below(dl[c], 40) + STEP * (wave_d + fs[1, 9 + c])
        na = below(ad[c], 40) + STEP * (wave_a + fs[2, 9 + c] + obs * nd)
        out_d[c] = nd[0:NN]
        out_a[c] = na[0:NN]
        if c < 3:
            gb = gb + na * fs[0, c]
        else:
            gm = gm + na * mu(0, c - 3)
            if c < 6:
                tr = tr + na
    fine_grad = (STEP * gb, STEP * tr * lam0, STEP * gm)

    pm144 = lanes3(pm, 48)
    rst[...] = jnp.zeros_like(rst)
    for p in range(3):
        r = nn(pm144, rows3(below(fine_grad[p], 48)))
        rst[p * 10:(p + 1) * 10, :] = jnp.sum(r.reshape(10, 8, E) * mask[None], axis=1)
    wh, wl = split(jnp.where(slot, jnp.concatenate([rst[...]] * 4, axis=0), 0.0))
    pt_s.reshape(ND, 128)[...] = nt(u, wh) + nt(u, wl)
    send_rows(pt_s, pt_r, 3)
    wait_rows(pt_r, rsem.at[3])
    gh, gl = split(pt_r.reshape(ND, 128)[...])
    total = jnp.where(same, tn(gh, asked) + tn(gl, asked), 0.0)
    total = total[0:32] + total[32:64] + total[64:96] + total[96:128]
    total = total[:, 0:32] + total[:, 32:64] + total[:, 64:96] + total[:, 96:128]
    out_h[...] = total[0:30] + reg[...] * coarse[...]

    wait_rows(rq_s, ssem.at[0])
    part = tr_s.at[:, pl.ds(0, NW - 1)]
    pltpu.make_async_copy(part, part, ssem.at[1]).wait()
    wait_rows(an_s, ssem.at[2])
    wait_rows(pt_s, ssem.at[3])


def place(*refs):
    sem = refs[-1]
    copies = [pltpu.make_async_copy(refs[at], refs[3 + at], sem.at[at]) for at in range(3)]
    for copy in copies:
        copy.start()
    for copy in copies:
        copy.wait()


def body(
    state0, delta, adjoint, model, geometry, normals, face_scale, derivative, lift, prolong, coarse_step, reg_weight,
    observe, owner, coarse_local, child, neighbor, orient, send_face,
):
    pick, turn = constants()
    ops = (
        state0, delta, adjoint, model, geometry, normals, face_scale, derivative,
        lift.transpose(2, 0, 1), prolong.transpose(2, 0, 1), coarse_step, reg_weight, observe,
        owner.reshape(1, E), coarse_local.reshape(1, E), child.reshape(1, E), neighbor, orient, send_face.reshape(1, 128),
        jnp.asarray(pick, bf16), jnp.asarray(turn),
    )
    vmem = pl.BlockSpec(memory_space=pltpu.VMEM)
    anywhere = pl.BlockSpec(memory_space=pl.ANY)
    hbm = pl.BlockSpec(memory_space=pltpu.HBM)
    row = pltpu.VMEM((ND, 1, 128), f32)
    results = (
        jax.ShapeDtypeStruct((NF, NN, E), f32),
        jax.ShapeDtypeStruct((NF, NN, E), f32),
        jax.ShapeDtypeStruct((30, 32), f32),
    )
    found = pl.pallas_call(
        kernel,
        out_shape=results,
        in_specs=[hbm] * len(ops),
        out_specs=(vmem, vmem, vmem),
        scratch_shapes=[
            *(pltpu.VMEM(op.shape, op.dtype) for op in ops),
            pltpu.VMEM((2, ROWS, TAB), bf16),
            pltpu.VMEM((TAB, OWN), bf16),
            pltpu.VMEM((27, 120, E), f32),
            pltpu.VMEM((ROWS, OWN), f32),
            pltpu.VMEM((4, 8, OWN), f32),
            pltpu.VMEM((18, 192, E), bf16),
            pltpu.VMEM((3, 18, 40, E), f32),
            pltpu.VMEM((64, 128), f32),
            pltpu.VMEM((32, E), f32),
            pltpu.VMEM((248, 144), bf16),
            pltpu.VMEM((4, NW, 4, 128), f32),
            pltpu.VMEM((4, NW, 4, 128), f32),
            row, row, row, row, row, row,
            pltpu.SemaphoreType.DMA((4,)),
            pltpu.SemaphoreType.DMA((4,)),
            pltpu.SemaphoreType.DMA((N_OPS,)),
        ],
        compiler_params=pltpu.CompilerParams(
            collective_id=0, has_side_effects=True, vmem_limit_bytes=60 * 1024 * 1024
        ),
    )(*ops)
    return pl.pallas_call(
        place,
        out_shape=results,
        in_specs=[anywhere] * 3,
        out_specs=(hbm, hbm, hbm),
        scratch_shapes=[pltpu.SemaphoreType.DMA((3,))],
        compiler_params=pltpu.CompilerParams(vmem_limit_bytes=60 * 1024 * 1024),
    )(*found)


def solution(mesh):
    both = ("region", "wave")
    placed = (
        P(None, None, both), P(None, None, both), P(None, None, both), P(None, None, both), P(None, both),
        P(None, None, both), P(None, both), P(), P(), P(), P(None, both), P(None, both), P(None, both),
        P(both, None), P(both), P(both), P(None, both), P(None, both), P(both),
    )
    return jax.shard_map(
        body, mesh=mesh, in_specs=placed,
        out_specs=(P(None, None, both), P(None, None, both), P(None, both)), check_vma=False,
    )
```

```python
import functools

import jax
import jax.numpy as jnp
import numpy as np
from jax import lax
from jax.experimental import pallas as pl
from jax.experimental.pallas import tpu as pltpu
from jax.sharding import PartitionSpec as P

f32, bf16, i32, i16 = jnp.float32, jnp.bfloat16, jnp.int32, jnp.int16
MESH = pl.DeviceIdType.MESH

STEP = 0.2
STRESS = ((0, 5, 4), (5, 1, 3), (4, 3, 2))
OFF = ((1, 2), (0, 2), (0, 1))
NF, NN, E, NW, ND = 9, 35, 256, 32, 128
OWN, TAB = 1024, 1152
ROWS = 27 * 16


def tables():
    triangle = [(a, b) for a in range(5) for b in range(5 - a)]
    nodes = [(a, b, c) for a in range(5) for b in range(5 - a) for c in range(5 - a - b)]
    face = np.zeros((4, 15), np.int32)
    for at, (a, b) in enumerate(triangle):
        for f, key in enumerate(((a, b, 0), (a, 0, b), (0, a, b), (a, b, 4 - a - b))):
            face[f, at] = nodes.index(key)
    orders = [(0, 1, 2), (1, 2, 0), (2, 0, 1), (0, 2, 1), (2, 1, 0), (1, 0, 2)]
    turning = np.zeros((6, 15), np.int32)
    for o, order in enumerate(orders):
        for at, (a, b) in enumerate(triangle):
            triple = (a, b, 4 - a - b)
            turning[o, at] = triangle.index((triple[order[0]], triple[order[1]]))
    return face, turning


def constants():
    face, turning = tables()
    pick = np.zeros((128, 144), np.float32)
    for f in range(4):
        for m in range(15):
            pick[f * 16 + m, face[f, m]] = 1.0
            pick[64 + f * 16 + m, 48 + face[f, m]] = 1.0
    turn = np.full((16, 128), 15, np.int32)
    for o in range(6):
        turn[:15, o] = turning[o]
    return pick, turn


def split(x):
    hi = x.astype(bf16)
    lo = (x - hi.astype(f32)).astype(bf16)
    return hi, lo


def nn(a, b):
    return lax.dot_general(a, b, (((1,), (0,)), ((), ())), preferred_element_type=f32)


def nt(a, b):
    return lax.dot_general(a, b, (((1,), (1,)), ((), ())), preferred_element_type=f32)


def tn(a, b):
    return lax.dot_general(a, b, (((0,), (0,)), ((), ())), preferred_element_type=f32)


def iota(shape, dim, kind=i32):
    return lax.broadcasted_iota(kind, shape, dim)


def below(x, rows):
    return jnp.concatenate([x, jnp.zeros((rows - x.shape[0], x.shape[1]), x.dtype)], axis=0)


def lanes3(x, width):
    hi = x.astype(bf16).astype(f32)
    lo = x - hi
    zero = jnp.zeros((x.shape[0], width - x.shape[1]), f32)
    return jnp.concatenate([hi, zero, hi, zero, lo, zero], axis=1).astype(bf16)


def rows3(x):
    hi, lo = split(x)
    return jnp.concatenate([hi, lo, hi], axis=0)


N_OPS = 21


def kernel(*refs):
    sources, (out_d, out_a, out_h) = refs[:N_OPS], refs[N_OPS:N_OPS + 3]
    held = refs[N_OPS + 3:2 * N_OPS + 3]
    isem = refs[-1]
    loads = [pltpu.make_async_copy(a, b, isem.at[at]) for at, (a, b) in enumerate(zip(sources, held))]
    for load in loads:
        load.start()
    work(loads, *held, out_d, out_a, out_h, *refs[2 * N_OPS + 3:-1])


def work(
    loads,
    s0, dl, ad, model, geometry, normals, face_scale, derivative, lift, prolong, coarse, reg, observe,
    owner, local, child, neighbor, orient, send_face, pick, turn,
    out_d, out_a, out_h,
    tab, hot, dq, jump, hn, xl, fs, ltr, rst, c1,
    tr_s, tr_r, ag_s, ag_r, p1, p2, p3, chot, new_d, new_a,
    ssem, rsem, osem,
):
    region, wave = lax.axis_index("region"), lax.axis_index("wave")
    me = region * NW + wave
    core = lax.rem(wave, 2)
    chip = lax.div(me, 2)
    barrier = pltpu.get_barrier_semaphore()

    def greet(there):
        pl.semaphore_signal(barrier, inc=1, device_id=there, device_id_type=MESH)

    def alike(i):
        d = lax.rem(me + 2 * i, ND)
        return lax.div(d, 2), (lax.div(d, NW), lax.rem(d, NW))

    def each(low, high, act):
        def one(i, c):
            act(i)
            return c

        lax.fori_loop(low, high, one, 0)

    sibling = (region, wave + 1 - 2 * core)
    each(0, 16, lambda i: greet((region, lax.rem(wave + 2 * i + 1, NW))))
    each(1, 64, lambda i: greet(alike(i)[1]))

    def send(src, dst, at, there):
        pltpu.make_async_remote_copy(
            src_ref=src, dst_ref=dst, send_sem=ssem.at[at], recv_sem=rsem.at[at], device_id=there, device_id_type=MESH
        ).start()

    def wait(part, sem):
        pltpu.make_async_copy(part, part, sem).wait()

    for load in loads:
        load.wait()

    cs = jnp.concatenate([coarse[...], jnp.zeros((2, 32), f32)], axis=0)
    cst = jnp.concatenate([cs, jnp.zeros((32, 96), f32)], axis=1).T
    ag_s[...] = jnp.concatenate([cst[q * 8:q * 8 + 8, 0:32] for q in range(4)], axis=1)
    ag_r[pl.ds(chip, 1), pl.ds(core, 1)] = ag_s[...].reshape(1, 1, 8, 128)

    u = (iota((ND, E), 0) == owner[...]).astype(f32).astype(bf16)
    ub = u.astype(f32)
    tri = (iota((E, E), 0) < iota((E, E), 1)).astype(f32).astype(bf16)
    before = jnp.sum(nn(u, tri) * ub, axis=0, keepdims=True).astype(i32)

    for k in range(3):
        c1[k * 40:(k + 1) * 40, :] = lanes3(below(derivative[k], 40), 48)
    c1[120:248, :] = pick[...]
    for s, ref in enumerate((s0, dl, ad)):
        for c in range(NF):
            sc = s * NF + c
            got = nn(c1[...], rows3(below(ref[c], 48)))
            dq[sc] = got[0:120]
            for f in range(4):
                span = slice(f * E, (f + 1) * E)
                tab[0, sc * 16:(sc + 1) * 16, span] = got[120 + f * 16:136 + f * 16].astype(bf16)
                tab[1, sc * 16:(sc + 1) * 16, span] = got[184 + f * 16:200 + f * 16].astype(bf16)

    pickt = (iota((OWN, 128), 0) == send_face[...]).astype(f32).astype(bf16)
    sent = nn(tab[0, :, 0:OWN], pickt) + nn(tab[1, :, 0:OWN], pickt)
    sent = below(sent, 512)
    for j in range(4):
        tr_s.reshape(4, 128, 128)[j] = sent[j * 128:(j + 1) * 128].T

    pl.semaphore_wait(barrier, 79)

    def send_trace(i):
        w = lax.rem(wave + i, NW)
        send(tr_s.at[:, pl.ds(w, 1)], tr_r.at[:, pl.ds(wave, 1)], 0, (region, w))

    each(1, NW, send_trace)
    each(1, 64, lambda i: send(ag_s, ag_r.at[chip, core], 1, alike(i)[1]))
    tr_r[:, pl.ds(wave, 1)] = tr_s[:, pl.ds(wave, 1)]

    for f in range(4):
        row = neighbor[f:f + 1, :].astype(i16)
        hot[:, f * E:(f + 1) * E] = jnp.where(
            iota((TAB, E), 0, i16) == row, jnp.ones((), bf16), jnp.zeros((), bf16)
        )

    line = (owner[...] * 8 + (local[...] & 7)).astype(i16)
    chot[...] = jnp.where(iota((1024, E), 0, i16) == line, jnp.ones((), bf16), jnp.zeros((), bf16))

    for f in range(4):
        span = slice(f * E, (f + 1) * E)
        jump[:, span] = nn(tab[0, :, 0:OWN], hot[0:OWN, span]) + nn(tab[1, :, 0:OWN], hot[0:OWN, span])

    wait(ag_r.at[pl.ds(0, 63), 0], rsem.at[1])
    send(ag_r.at[:, pl.ds(core, 1)], ag_r.at[:, pl.ds(core, 1)], 2, sibling)

    wait(tr_r.at[:, pl.ds(0, NW - 1)], rsem.at[0])
    for j in range(4):
        rows = min(128, ROWS - j * 128)
        hi, lo = split(tr_r.reshape(4, 128, 128)[j].T[0:rows])
        tab[0, j * 128:j * 128 + rows, OWN:TAB] = hi
        tab[1, j * 128:j * 128 + rows, OWN:TAB] = lo
    for f in range(4):
        span = slice(f * E, (f + 1) * E)
        jump[:, span] += nn(tab[0, :, OWN:TAB], hot[OWN:TAB, span]) + nn(tab[1, :, OWN:TAB], hot[OWN:TAB, span])

    for f in range(4):
        span = slice(f * E, (f + 1) * E)
        h = 0.5 * face_scale[f:f + 1, :]
        for j in range(3):
            hn[j, :, span] = jnp.broadcast_to(h * normals[j, f:f + 1, :], (8, E))
        hn[3, :, span] = jnp.broadcast_to(h, (8, E))

    ltr[...] = jnp.zeros_like(ltr)
    for f in range(4):
        for m in range(15):
            ltr[f * 16 + m:f * 16 + m + 1, 0:NN] = lift[m, f:f + 1, :]
    lh, ll = split(ltr[...].T[0:40])
    lmat = jnp.concatenate([lh.astype(f32), lh.astype(f32), ll.astype(f32)], axis=1).astype(bf16)

    for f in range(4):
        span = slice(f * E, (f + 1) * E)
        o = orient[f:f + 1, :]
        idx = jnp.full((16, E), 15, i32)
        for q in range(6):
            idx = jnp.where(o == q, turn[:, q:q + 1], idx)
        low = idx < 8
        idx = idx & 7
        ia, ib = idx[0:8], idx[8:16]
        for sc in range(27):
            a = jump[sc * 16:sc * 16 + 8, span]
            b = jump[sc * 16 + 8:sc * 16 + 16, span]
            own = tab[0, sc * 16:sc * 16 + 16, span].astype(f32) + tab[1, sc * 16:sc * 16 + 16, span].astype(f32)
            for t, ix in enumerate((ia, ib)):
                ga = jnp.take_along_axis(a, ix, axis=0, mode="promise_in_bounds")
                gb = jnp.take_along_axis(b, ix, axis=0, mode="promise_in_bounds")
                jump[sc * 16 + t * 8:sc * 16 + t * 8 + 8, span] = (
                    jnp.where(low[t * 8:t * 8 + 8], ga, gb) - own[t * 8:t * 8 + 8]
                )

    geo = [geometry[q:q + 1, :] for q in range(9)]

    def grad(sc, i):
        return sum(geo[3 * i + k] * dq[sc, k * 40:(k + 1) * 40, :] for k in range(3))

    for s in range(3):
        for f in range(4):
            span = slice(f * E, (f + 1) * E)
            n = [jnp.concatenate([hn[j, :, span]] * 2, axis=0) for j in range(4)]
            q = [jump[(s * NF + c) * 16:(s * NF + c) * 16 + 16, span] for c in range(NF)]
            chans = [sum(n[j] * q[3 + STRESS[i][j]] for j in range(3)) for i in range(3)]
            chans += [n[j] * q[j] for j in range(3)]
            chans += [n[i] * q[j] + n[j] * q[i] for i, j in OFF]
            if s > 0:
                chans += [n[3] * q[c] for c in range(NF)]
            for at, g in enumerate(chans):
                hi, lo = split(g)
                xl[at, f * 16:f * 16 + 16, :] = hi
                xl[at, 64 + f * 16:80 + f * 16, :] = lo
                xl[at, 128 + f * 16:144 + f * 16, :] = hi
        base = s * NF
        for i in range(3):
            fs[s, i] = nn(lmat, xl[i]) + sum(grad(base + 3 + STRESS[i][j], j) for j in range(3))
            fs[s, 3 + i] = nn(lmat, xl[3 + i]) + grad(base + i, i)
        for at, (i, j) in enumerate(OFF):
            fs[s, 6 + at] = nn(lmat, xl[6 + at]) + grad(base + j, i) + grad(base + i, j)
        if s > 0:
            for c in range(NF):
                fs[s, 9 + c] = nn(lmat, xl[9 + c])

    wait(ag_r.at[:, pl.ds(0, 1)], rsem.at[2])
    chi, clo = split(ag_r[...].reshape(1024, 128).T)
    found = jnp.where(
        lax.div(iota((128, E), 0), 32) == lax.shift_right_logical(local[...], 3), nn(chi, chot[...]) + nn(clo, chot[...]), 0.0
    )
    found = found[0:32] + found[32:64] + found[64:96] + found[96:128]
    mask = (iota((8, E), 0) == child[...]).astype(f32)
    pm = prolong[...].reshape(80, NN)
    pm40 = jnp.concatenate([pm, jnp.zeros((80, 5), f32)], axis=1)
    ph, pw = split(pm40)
    pm3 = jnp.concatenate([ph, ph, pw], axis=0)
    fine = []
    for p in range(3):
        z = jnp.concatenate([mask * found[p * 10 + k:p * 10 + k + 1, :] for k in range(10)], axis=0)
        fine.append(tn(pm3, rows3(z)))

    m0, m1, m2 = (below(model[p], 40) for p in range(3))

    def lam(s):
        return fs[s, 3] + fs[s, 4] + fs[s, 5]

    def mu(s, k):
        return 2.0 * fs[s, 3 + k] if k < 3 else fs[s, 3 + k]

    lam0 = lam(0)
    lam1 = m1 * lam(1) + fine[1] * lam0
    lam2 = m1 * lam(2)
    obs = below(observe[...], 40)
    gb = jnp.zeros((40, E), f32)
    tr = jnp.zeros((40, E), f32)
    gm = jnp.zeros((40, E), f32)
    for c in range(NF):
        if c < 3:
            wave_d = m0 * fs[1, c] + fine[0] * fs[0, c]
            wave_a = m0 * fs[2, c]
        else:
            wave_d = m2 * mu(1, c - 3) + fine[2] * mu(0, c - 3)
            wave_a = m2 * mu(2, c - 3)
            if c < 6:
                wave_d = wave_d + lam1
                wave_a = wave_a + lam2
        nd = below(dl[c], 40) + STEP * (wave_d + fs[1, 9 + c])
        na = below(ad[c], 40) + STEP * (wave_a + fs[2, 9 + c] + obs * nd)
        new_d[c] = nd[0:NN]
        new_a[c] = na[0:NN]
        if c < 3:
            gb = gb + na * fs[0, c]
        else:
            gm = gm + na * mu(0, c - 3)
            if c < 6:
                tr = tr + na
    stores = [pltpu.make_async_copy(new_d, out_d, osem.at[0]), pltpu.make_async_copy(new_a, out_a, osem.at[1])]
    for store in stores:
        store.start()
    fine_grad = (STEP * gb, STEP * tr * lam0, STEP * gm)

    pm144 = lanes3(pm, 48)
    rst[30:31, :] = local[...].astype(f32)
    rst[31:32, :] = jnp.zeros((1, E), f32)
    for p in range(3):
        r = nn(pm144, rows3(below(fine_grad[p], 48)))
        rst[p * 10:(p + 1) * 10, :] = jnp.sum(r.reshape(10, 8, E) * mask[None], axis=1)
    slot = lax.div(iota((128, E), 0), 32) == before
    wh, wl = split(jnp.where(slot, jnp.concatenate([rst[...]] * 4, axis=0), 0.0))
    p1.reshape(ND, 128)[...] = nt(u, wh) + nt(u, wl)
    send(p1.at[:, pl.ds(1 - core, 1)], p2.at[:, pl.ds(core, 1)], 3, sibling)
    p2[:, pl.ds(core, 1)] = p1[:, pl.ds(core, 1)]
    wait(p2.at[:, pl.ds(0, 1)], rsem.at[3])

    def send_partial(i):
        to, there = alike(i)
        send(p2.at[to], p3.at[chip], 4, there)

    each(1, 64, send_partial)
    p3[pl.ds(chip, 1)] = p2[pl.ds(chip, 1)]
    wait(p3.at[pl.ds(0, 63)], rsem.at[4])
    gh, gl = split(p3.reshape(ND, 128)[...])
    place_of = lax.rem(iota((128, 128), 1), 32)
    spread = (iota((128, 128), 0) == iota((128, 128), 1) - place_of + 30).astype(f32).astype(bf16)
    asked = (nn(gh, spread).astype(i32) == place_of).astype(f32).astype(bf16)
    same = lax.div(iota((128, 128), 0), 32) == lax.div(iota((128, 128), 1), 32)
    total = jnp.where(same, tn(gh, asked) + tn(gl, asked), 0.0)
    total = total[0:32] + total[32:64] + total[64:96] + total[96:128]
    total = total[:, 0:32] + total[:, 32:64] + total[:, 64:96] + total[:, 96:128]
    out_h[...] = total[0:30] + reg[...] * coarse[...]

    wait(tr_s.at[:, pl.ds(0, NW - 1)], ssem.at[0])
    wait(ag_r.at[pl.ds(0, 63), 0], ssem.at[1])
    wait(ag_r.at[:, pl.ds(0, 1)], ssem.at[2])
    wait(p1.at[:, pl.ds(0, 1)], ssem.at[3])
    wait(p2.at[pl.ds(0, 63)], ssem.at[4])
    for store in stores:
        store.wait()


def place(*refs):
    isem, osem = refs[-2:]
    loads = [pltpu.make_async_copy(refs[at], refs[6 + at], isem.at[at]) for at in range(3)]
    stores = [pltpu.make_async_copy(refs[6 + at], refs[3 + at], osem.at[at]) for at in range(3)]
    for load in loads:
        load.start()
    for load, store in zip(loads, stores):
        load.wait()
        store.start()
    for store in stores:
        store.wait()


def body(
    state0, delta, adjoint, model, geometry, normals, face_scale, derivative, lift, prolong, coarse_step, reg_weight,
    observe, owner, coarse_local, child, neighbor, orient, send_face,
):
    pick, turn = constants()
    ops = (
        state0, delta, adjoint, model, geometry, normals, face_scale, derivative,
        lift.transpose(2, 0, 1), prolong.transpose(2, 0, 1), coarse_step, reg_weight, observe,
        owner.reshape(1, E), coarse_local.reshape(1, E), child.reshape(1, E), neighbor, orient, send_face.reshape(1, 128),
        jnp.asarray(pick, bf16), jnp.asarray(turn),
    )
    vmem = pl.BlockSpec(memory_space=pltpu.VMEM)
    anywhere = pl.BlockSpec(memory_space=pl.ANY)
    hbm = pl.BlockSpec(memory_space=pltpu.HBM)
    row = pltpu.VMEM((64, 2, 1, 128), f32)
    results = (
        jax.ShapeDtypeStruct((NF, NN, E), f32),
        jax.ShapeDtypeStruct((NF, NN, E), f32),
        jax.ShapeDtypeStruct((30, 32), f32),
    )
    found = pl.pallas_call(
        kernel,
        out_shape=results,
        in_specs=[hbm] * len(ops),
        out_specs=(hbm, hbm, vmem),
        scratch_shapes=[
            *(pltpu.VMEM(op.shape, op.dtype) for op in ops),
            pltpu.VMEM((2, ROWS, TAB), bf16),
            pltpu.VMEM((TAB, OWN), bf16),
            pltpu.VMEM((27, 120, E), f32),
            pltpu.VMEM((ROWS, OWN), f32),
            pltpu.VMEM((4, 8, OWN), f32),
            pltpu.VMEM((18, 192, E), bf16),
            pltpu.VMEM((3, 18, 40, E), f32),
            pltpu.VMEM((64, 128), f32),
            pltpu.VMEM((32, E), f32),
            pltpu.VMEM((248, 144), bf16),
            pltpu.VMEM((4, NW, 4, 128), f32),
            pltpu.VMEM((4, NW, 4, 128), f32),
            pltpu.VMEM((8, 128), f32),
            pltpu.VMEM((64, 2, 8, 128), f32),
            row, row, row,
            pltpu.VMEM((1024, E), bf16),
            pltpu.VMEM((NF, NN, E), f32),
            pltpu.VMEM((NF, NN, E), f32),
            pltpu.SemaphoreType.DMA((5,)),
            pltpu.SemaphoreType.DMA((5,)),
            pltpu.SemaphoreType.DMA((2,)),
            pltpu.SemaphoreType.DMA((N_OPS,)),
        ],
        compiler_params=pltpu.CompilerParams(
            collective_id=0, has_side_effects=True, vmem_limit_bytes=60 * 1024 * 1024
        ),
    )(*ops)
    return pl.pallas_call(
        place,
        out_shape=results,
        in_specs=[anywhere] * 3,
        out_specs=(hbm, hbm, hbm),
        scratch_shapes=[
            *(pltpu.VMEM(r.shape, r.dtype) for r in results),
            pltpu.SemaphoreType.DMA((3,)),
            pltpu.SemaphoreType.DMA((3,)),
        ],
        compiler_params=pltpu.CompilerParams(vmem_limit_bytes=60 * 1024 * 1024),
    )(*found)


def solution(mesh):
    both = ("region", "wave")
    placed = (
        P(None, None, both), P(None, None, both), P(None, None, both), P(None, None, both), P(None, both),
        P(None, None, both), P(None, both), P(), P(), P(), P(None, both), P(None, both), P(None, both),
        P(both, None), P(both), P(both), P(None, both), P(None, both), P(both),
    )
    return jax.shard_map(
        body, mesh=mesh, in_specs=placed,
        out_specs=(P(None, None, both), P(None, None, both), P(None, both)), check_vma=False,
    )
```

```python
import functools

import jax
import jax.numpy as jnp
import numpy as np
from jax import lax
from jax.experimental import pallas as pl
from jax.experimental.pallas import tpu as pltpu
from jax.sharding import PartitionSpec as P

f32, bf16, i32, i16 = jnp.float32, jnp.bfloat16, jnp.int32, jnp.int16
MESH = pl.DeviceIdType.MESH

STEP = 0.2
STRESS = ((0, 5, 4), (5, 1, 3), (4, 3, 2))
OFF = ((1, 2), (0, 2), (0, 1))
NF, NN, E, NW, ND = 9, 35, 256, 32, 128
OWN, TAB = 1024, 1152
ROWS = 27 * 16


def tables():
    triangle = [(a, b) for a in range(5) for b in range(5 - a)]
    nodes = [(a, b, c) for a in range(5) for b in range(5 - a) for c in range(5 - a - b)]
    face = np.zeros((4, 15), np.int32)
    for at, (a, b) in enumerate(triangle):
        for f, key in enumerate(((a, b, 0), (a, 0, b), (0, a, b), (a, b, 4 - a - b))):
            face[f, at] = nodes.index(key)
    orders = [(0, 1, 2), (1, 2, 0), (2, 0, 1), (0, 2, 1), (2, 1, 0), (1, 0, 2)]
    turning = np.zeros((6, 15), np.int32)
    for o, order in enumerate(orders):
        for at, (a, b) in enumerate(triangle):
            triple = (a, b, 4 - a - b)
            turning[o, at] = triangle.index((triple[order[0]], triple[order[1]]))
    return face, turning


def constants():
    face, turning = tables()
    pick = np.zeros((128, 144), np.float32)
    for f in range(4):
        for m in range(15):
            pick[f * 16 + m, face[f, m]] = 1.0
            pick[64 + f * 16 + m, 48 + face[f, m]] = 1.0
    turn = np.full((16, 128), 15, np.int32)
    for o in range(6):
        turn[:15, o] = turning[o]
    return pick, turn


def split(x):
    hi = x.astype(bf16)
    lo = (x - hi.astype(f32)).astype(bf16)
    return hi, lo


def nn(a, b):
    return lax.dot_general(a, b, (((1,), (0,)), ((), ())), preferred_element_type=f32)


def nt(a, b):
    return lax.dot_general(a, b, (((1,), (1,)), ((), ())), preferred_element_type=f32)


def tn(a, b):
    return lax.dot_general(a, b, (((0,), (0,)), ((), ())), preferred_element_type=f32)


def iota(shape, dim, kind=i32):
    return lax.broadcasted_iota(kind, shape, dim)


def below(x, rows):
    return jnp.concatenate([x, jnp.zeros((rows - x.shape[0], x.shape[1]), x.dtype)], axis=0)


def lanes3(x, width):
    hi = x.astype(bf16).astype(f32)
    lo = x - hi
    zero = jnp.zeros((x.shape[0], width - x.shape[1]), f32)
    return jnp.concatenate([hi, zero, hi, zero, lo, zero], axis=1).astype(bf16)


def rows3(x):
    hi, lo = split(x)
    return jnp.concatenate([hi, lo, hi], axis=0)


N_OPS = 21


def kernel(*refs):
    sources, (out_d, out_a, out_h) = refs[:N_OPS], refs[N_OPS:N_OPS + 3]
    held = refs[N_OPS + 3:2 * N_OPS + 3]
    isem = refs[-1]
    loads = [pltpu.make_async_copy(a, b, isem.at[at]) for at, (a, b) in enumerate(zip(sources, held))]
    for load in loads:
        load.start()
    work(loads, *held, out_d, out_a, out_h, *refs[2 * N_OPS + 3:-1])


def work(
    loads,
    s0, dl, ad, model, geometry, normals, face_scale, derivative, lift, prolong, coarse, reg, observe,
    owner, local, child, neighbor, orient, send_face, pick, turn,
    out_d, out_a, out_h,
    tab, hot, dq, jump, hn, xl, fs, ltr, rst, c1,
    tr_s, tr_r, ag_s, ag_r, p1, p2, p3, chot, new_d, new_a, lmat, order,
    ssem, rsem, osem,
):
    region, wave = lax.axis_index("region"), lax.axis_index("wave")
    me = region * NW + wave
    core = lax.rem(wave, 2)
    chip = lax.div(me, 2)
    barrier = pltpu.get_barrier_semaphore()

    def greet(there):
        pl.semaphore_signal(barrier, inc=1, device_id=there, device_id_type=MESH)

    def alike(i):
        d = lax.rem(me + 2 * i, ND)
        return lax.div(d, 2), (lax.div(d, NW), lax.rem(d, NW))

    def each(low, high, act):
        def one(i, c):
            act(i)
            return c

        lax.fori_loop(low, high, one, 0)

    sibling = (region, wave + 1 - 2 * core)
    each(0, 16, lambda i: greet((region, lax.rem(wave + 2 * i + 1, NW))))
    each(1, 64, lambda i: greet(alike(i)[1]))

    def send(src, dst, at, there):
        pltpu.make_async_remote_copy(
            src_ref=src, dst_ref=dst, send_sem=ssem.at[at], recv_sem=rsem.at[at], device_id=there, device_id_type=MESH
        ).start()

    def wait(part, sem):
        pltpu.make_async_copy(part, part, sem).wait()

    for load in loads:
        load.wait()

    cs = jnp.concatenate([coarse[...], jnp.zeros((2, 32), f32)], axis=0)
    cst = jnp.concatenate([cs, jnp.zeros((32, 96), f32)], axis=1).T
    ag_s[...] = jnp.concatenate([cst[q * 8:q * 8 + 8, 0:32] for q in range(4)], axis=1)
    ag_r[pl.ds(chip, 1), pl.ds(core, 1)] = ag_s[...].reshape(1, 1, 8, 128)

    u = (iota((ND, E), 0) == owner[...]).astype(f32).astype(bf16)
    ub = u.astype(f32)
    tri = (iota((E, E), 0) < iota((E, E), 1)).astype(f32).astype(bf16)
    before = jnp.sum(nn(u, tri) * ub, axis=0, keepdims=True).astype(i32)

    for k in range(3):
        c1[k * 40:(k + 1) * 40, :] = lanes3(below(derivative[k], 40), 48)
    c1[120:248, :] = pick[...]
    for s, ref in enumerate((s0, dl, ad)):
        for c in range(NF):
            sc = s * NF + c
            got = nn(c1[...], rows3(below(ref[c], 48)))
            dq[sc] = got[0:120]
            for f in range(4):
                span = slice(f * E, (f + 1) * E)
                tab[0, sc * 16:(sc + 1) * 16, span] = got[120 + f * 16:136 + f * 16].astype(bf16)
                tab[1, sc * 16:(sc + 1) * 16, span] = got[184 + f * 16:200 + f * 16].astype(bf16)

    pickt = (iota((OWN, 128), 0) == send_face[...]).astype(f32).astype(bf16)
    sent = nn(tab[0, :, 0:OWN], pickt) + nn(tab[1, :, 0:OWN], pickt)
    sent = below(sent, 512)
    for j in range(4):
        tr_s.reshape(4, 128, 128)[j] = sent[j * 128:(j + 1) * 128].T

    pl.semaphore_wait(barrier, 79)

    def send_trace(i):
        w = lax.rem(wave + i, NW)
        send(tr_s.at[:, pl.ds(w, 1)], tr_r.at[:, pl.ds(wave, 1)], 0, (region, w))

    each(1, NW, send_trace)
    each(1, 64, lambda i: send(ag_s, ag_r.at[chip, core], 1, alike(i)[1]))
    tr_r[:, pl.ds(wave, 1)] = tr_s[:, pl.ds(wave, 1)]

    for f in range(4):
        row = neighbor[f:f + 1, :].astype(i16)
        hot[:, f * E:(f + 1) * E] = jnp.where(
            iota((TAB, E), 0, i16) == row, jnp.ones((), bf16), jnp.zeros((), bf16)
        )

    line = (owner[...] * 8 + (local[...] & 7)).astype(i16)
    chot[...] = jnp.where(iota((1024, E), 0, i16) == line, jnp.ones((), bf16), jnp.zeros((), bf16))

    for f in range(4):
        span = slice(f * E, (f + 1) * E)
        jump[:, span] = nn(tab[0, :, 0:OWN], hot[0:OWN, span]) + nn(tab[1, :, 0:OWN], hot[0:OWN, span])

    for f in range(4):
        span = slice(f * E, (f + 1) * E)
        h = 0.5 * face_scale[f:f + 1, :]
        for j in range(3):
            hn[j, :, span] = jnp.broadcast_to(h * normals[j, f:f + 1, :], (8, E))
        hn[3, :, span] = jnp.broadcast_to(h, (8, E))

    ltr[...] = jnp.zeros_like(ltr)
    for f in range(4):
        for m in range(15):
            ltr[f * 16 + m:f * 16 + m + 1, 0:NN] = lift[m, f:f + 1, :]
    lh, ll = split(ltr[...].T[0:40])
    lmat[...] = jnp.concatenate([lh.astype(f32), lh.astype(f32), ll.astype(f32)], axis=1).astype(bf16)

    for f in range(4):
        span = slice(f * E, (f + 1) * E)
        idx = jnp.full((16, E), 15, i32)
        for q in range(6):
            idx = jnp.where(orient[f:f + 1, :] == q, turn[:, q:q + 1], idx)
        order[:, span] = idx

    geo = [geometry[q:q + 1, :] for q in range(9)]

    def grad(sc, i):
        return sum(geo[3 * i + k] * dq[sc, k * 40:(k + 1) * 40, :] for k in range(3))

    for s in range(3):
        base = s * NF
        for i in range(3):
            fs[s, i] = sum(grad(base + 3 + STRESS[i][j], j) for j in range(3))
            fs[s, 3 + i] = grad(base + i, i)
        for at, (i, j) in enumerate(OFF):
            fs[s, 6 + at] = grad(base + j, i) + grad(base + i, j)

    mask = (iota((8, E), 0) == child[...]).astype(f32)
    pm = prolong[...].reshape(80, NN)
    pm40 = jnp.concatenate([pm, jnp.zeros((80, 5), f32)], axis=1)
    ph, pw = split(pm40)
    pm3 = jnp.concatenate([ph, ph, pw], axis=0)
    pm144 = lanes3(pm, 48)

    wait(tr_r.at[:, pl.ds(0, NW - 1)], rsem.at[0])
    for j in range(4):
        rows = min(128, ROWS - j * 128)
        hi, lo = split(tr_r.reshape(4, 128, 128)[j].T[0:rows])
        tab[0, j * 128:j * 128 + rows, OWN:TAB] = hi
        tab[1, j * 128:j * 128 + rows, OWN:TAB] = lo
    for f in range(4):
        span = slice(f * E, (f + 1) * E)
        jump[:, span] += nn(tab[0, :, OWN:TAB], hot[OWN:TAB, span]) + nn(tab[1, :, OWN:TAB], hot[OWN:TAB, span])

    for f in range(4):
        span = slice(f * E, (f + 1) * E)
        idx = order[:, span]
        low = idx < 8
        idx = idx & 7
        ia, ib = idx[0:8], idx[8:16]
        for sc in range(27):
            a = jump[sc * 16:sc * 16 + 8, span]
            b = jump[sc * 16 + 8:sc * 16 + 16, span]
            own = tab[0, sc * 16:sc * 16 + 16, span].astype(f32) + tab[1, sc * 16:sc * 16 + 16, span].astype(f32)
            for t, ix in enumerate((ia, ib)):
                ga = jnp.take_along_axis(a, ix, axis=0, mode="promise_in_bounds")
                gb = jnp.take_along_axis(b, ix, axis=0, mode="promise_in_bounds")
                jump[sc * 16 + t * 8:sc * 16 + t * 8 + 8, span] = (
                    jnp.where(low[t * 8:t * 8 + 8], ga, gb) - own[t * 8:t * 8 + 8]
                )

    def terms(s):
        for f in range(4):
            span = slice(f * E, (f + 1) * E)
            n = [jnp.concatenate([hn[j, :, span]] * 2, axis=0) for j in range(4)]
            q = [jump[(s * NF + c) * 16:(s * NF + c) * 16 + 16, span] for c in range(NF)]
            chans = [sum(n[j] * q[3 + STRESS[i][j]] for j in range(3)) for i in range(3)]
            chans += [n[j] * q[j] for j in range(3)]
            chans += [n[i] * q[j] + n[j] * q[i] for i, j in OFF]
            if s > 0:
                chans += [n[3] * q[c] for c in range(NF)]
            for at, g in enumerate(chans):
                hi, lo = split(g)
                xl[at, f * 16:f * 16 + 16, :] = hi
                xl[at, 64 + f * 16:80 + f * 16, :] = lo
                xl[at, 128 + f * 16:144 + f * 16, :] = hi
        for at in range(9):
            fs[s, at] += nn(lmat[...], xl[at])
        if s > 0:
            for at in range(9, 18):
                fs[s, at] = nn(lmat[...], xl[at])

    terms(0)

    wait(ag_r.at[pl.ds(0, 63), 0], rsem.at[1])
    send(ag_r.at[:, pl.ds(core, 1)], ag_r.at[:, pl.ds(core, 1)], 2, sibling)

    terms(1)
    terms(2)

    wait(ag_r.at[:, pl.ds(0, 1)], rsem.at[2])
    chi, clo = split(ag_r[...].reshape(1024, 128).T)
    found = jnp.where(
        lax.div(iota((128, E), 0), 32) == lax.shift_right_logical(local[...], 3), nn(chi, chot[...]) + nn(clo, chot[...]), 0.0
    )
    found = found[0:32] + found[32:64] + found[64:96] + found[96:128]
    fine = []
    for p in range(3):
        z = jnp.concatenate([mask * found[p * 10 + k:p * 10 + k + 1, :] for k in range(10)], axis=0)
        fine.append(tn(pm3, rows3(z)))

    m0, m1, m2 = (below(model[p], 40) for p in range(3))

    def lam(s):
        return fs[s, 3] + fs[s, 4] + fs[s, 5]

    def mu(s, k):
        return 2.0 * fs[s, 3 + k] if k < 3 else fs[s, 3 + k]

    lam0 = lam(0)
    lam1 = m1 * lam(1) + fine[1] * lam0
    lam2 = m1 * lam(2)
    obs = below(observe[...], 40)
    gb = jnp.zeros((40, E), f32)
    tr = jnp.zeros((40, E), f32)
    gm = jnp.zeros((40, E), f32)
    for c in range(NF):
        if c < 3:
            wave_d = m0 * fs[1, c] + fine[0] * fs[0, c]
            wave_a = m0 * fs[2, c]
        else:
            wave_d = m2 * mu(1, c - 3) + fine[2] * mu(0, c - 3)
            wave_a = m2 * mu(2, c - 3)
            if c < 6:
                wave_d = wave_d + lam1
                wave_a = wave_a + lam2
        nd = below(dl[c], 40) + STEP * (wave_d + fs[1, 9 + c])
        na = below(ad[c], 40) + STEP * (wave_a + fs[2, 9 + c] + obs * nd)
        new_d[c] = nd[0:NN]
        new_a[c] = na[0:NN]
        if c < 3:
            gb = gb + na * fs[0, c]
        else:
            gm = gm + na * mu(0, c - 3)
            if c < 6:
                tr = tr + na
    stores = [pltpu.make_async_copy(new_d, out_d, osem.at[0]), pltpu.make_async_copy(new_a, out_a, osem.at[1])]
    for store in stores:
        store.start()
    fine_grad = (STEP * gb, STEP * tr * lam0, STEP * gm)

    rst[30:31, :] = local[...].astype(f32)
    rst[31:32, :] = jnp.zeros((1, E), f32)
    for p in range(3):
        r = nn(pm144, rows3(below(fine_grad[p], 48)))
        rst[p * 10:(p + 1) * 10, :] = jnp.sum(r.reshape(10, 8, E) * mask[None], axis=1)
    slot = lax.div(iota((128, E), 0), 32) == before
    wh, wl = split(jnp.where(slot, jnp.concatenate([rst[...]] * 4, axis=0), 0.0))
    p1.reshape(ND, 128)[...] = nt(u, wh) + nt(u, wl)
    send(p1.at[:, pl.ds(1 - core, 1)], p2.at[:, pl.ds(core, 1)], 3, sibling)
    p2[:, pl.ds(core, 1)] = p1[:, pl.ds(core, 1)]
    wait(p2.at[:, pl.ds(0, 1)], rsem.at[3])

    def send_partial(i):
        to, there = alike(i)
        send(p2.at[to], p3.at[chip], 4, there)

    each(1, 64, send_partial)
    p3[pl.ds(chip, 1)] = p2[pl.ds(chip, 1)]
    wait(p3.at[pl.ds(0, 63)], rsem.at[4])
    gh, gl = split(p3.reshape(ND, 128)[...])
    place_of = lax.rem(iota((128, 128), 1), 32)
    spread = (iota((128, 128), 0) == iota((128, 128), 1) - place_of + 30).astype(f32).astype(bf16)
    asked = (nn(gh, spread).astype(i32) == place_of).astype(f32).astype(bf16)
    same = lax.div(iota((128, 128), 0), 32) == lax.div(iota((128, 128), 1), 32)
    total = jnp.where(same, tn(gh, asked) + tn(gl, asked), 0.0)
    total = total[0:32] + total[32:64] + total[64:96] + total[96:128]
    total = total[:, 0:32] + total[:, 32:64] + total[:, 64:96] + total[:, 96:128]
    out_h[...] = total[0:30] + reg[...] * coarse[...]

    wait(tr_s.at[:, pl.ds(0, NW - 1)], ssem.at[0])
    wait(ag_r.at[pl.ds(0, 63), 0], ssem.at[1])
    wait(ag_r.at[:, pl.ds(0, 1)], ssem.at[2])
    wait(p1.at[:, pl.ds(0, 1)], ssem.at[3])
    wait(p2.at[pl.ds(0, 63)], ssem.at[4])
    for store in stores:
        store.wait()


def place(*refs):
    isem, osem = refs[-2:]
    loads = [pltpu.make_async_copy(refs[at], refs[6 + at], isem.at[at]) for at in range(3)]
    stores = [pltpu.make_async_copy(refs[6 + at], refs[3 + at], osem.at[at]) for at in range(3)]
    for load in loads:
        load.start()
    for load, store in zip(loads, stores):
        load.wait()
        store.start()
    for store in stores:
        store.wait()


def body(
    state0, delta, adjoint, model, geometry, normals, face_scale, derivative, lift, prolong, coarse_step, reg_weight,
    observe, owner, coarse_local, child, neighbor, orient, send_face,
):
    pick, turn = constants()
    ops = (
        state0, delta, adjoint, model, geometry, normals, face_scale, derivative,
        lift.transpose(2, 0, 1), prolong.transpose(2, 0, 1), coarse_step, reg_weight, observe,
        owner.reshape(1, E), coarse_local.reshape(1, E), child.reshape(1, E), neighbor, orient, send_face.reshape(1, 128),
        jnp.asarray(pick, bf16), jnp.asarray(turn),
    )
    vmem = pl.BlockSpec(memory_space=pltpu.VMEM)
    anywhere = pl.BlockSpec(memory_space=pl.ANY)
    hbm = pl.BlockSpec(memory_space=pltpu.HBM)
    row = pltpu.VMEM((64, 2, 1, 128), f32)
    results = (
        jax.ShapeDtypeStruct((NF, NN, E), f32),
        jax.ShapeDtypeStruct((NF, NN, E), f32),
        jax.ShapeDtypeStruct((30, 32), f32),
    )
    found = pl.pallas_call(
        kernel,
        out_shape=results,
        in_specs=[hbm] * len(ops),
        out_specs=(hbm, hbm, vmem),
        scratch_shapes=[
            *(pltpu.VMEM(op.shape, op.dtype) for op in ops),
            pltpu.VMEM((2, ROWS, TAB), bf16),
            pltpu.VMEM((TAB, OWN), bf16),
            pltpu.VMEM((27, 120, E), f32),
            pltpu.VMEM((ROWS, OWN), f32),
            pltpu.VMEM((4, 8, OWN), f32),
            pltpu.VMEM((18, 192, E), bf16),
            pltpu.VMEM((3, 18, 40, E), f32),
            pltpu.VMEM((64, 128), f32),
            pltpu.VMEM((32, E), f32),
            pltpu.VMEM((248, 144), bf16),
            pltpu.VMEM((4, NW, 4, 128), f32),
            pltpu.VMEM((4, NW, 4, 128), f32),
            pltpu.VMEM((8, 128), f32),
            pltpu.VMEM((64, 2, 8, 128), f32),
            row, row, row,
            pltpu.VMEM((1024, E), bf16),
            pltpu.VMEM((NF, NN, E), f32),
            pltpu.VMEM((NF, NN, E), f32),
            pltpu.VMEM((40, 192), bf16),
            pltpu.VMEM((16, OWN), i32),
            pltpu.SemaphoreType.DMA((5,)),
            pltpu.SemaphoreType.DMA((5,)),
            pltpu.SemaphoreType.DMA((2,)),
            pltpu.SemaphoreType.DMA((N_OPS,)),
        ],
        compiler_params=pltpu.CompilerParams(
            collective_id=0, has_side_effects=True, vmem_limit_bytes=60 * 1024 * 1024
        ),
    )(*ops)
    return pl.pallas_call(
        place,
        out_shape=results,
        in_specs=[anywhere] * 3,
        out_specs=(hbm, hbm, hbm),
        scratch_shapes=[
            *(pltpu.VMEM(r.shape, r.dtype) for r in results),
            pltpu.SemaphoreType.DMA((3,)),
            pltpu.SemaphoreType.DMA((3,)),
        ],
        compiler_params=pltpu.CompilerParams(vmem_limit_bytes=60 * 1024 * 1024),
    )(*found)


def solution(mesh):
    both = ("region", "wave")
    placed = (
        P(None, None, both), P(None, None, both), P(None, None, both), P(None, None, both), P(None, both),
        P(None, None, both), P(None, both), P(), P(), P(), P(None, both), P(None, both), P(None, both),
        P(both, None), P(both), P(both), P(None, both), P(None, both), P(both),
    )
    return jax.shard_map(
        body, mesh=mesh, in_specs=placed,
        out_specs=(P(None, None, both), P(None, None, both), P(None, both)), check_vma=False,
    )
```

```python
import functools

import jax
import jax.numpy as jnp
import numpy as np
from jax import lax
from jax.experimental import pallas as pl
from jax.experimental.pallas import tpu as pltpu
from jax.sharding import PartitionSpec as P

f32, bf16, i32, i16 = jnp.float32, jnp.bfloat16, jnp.int32, jnp.int16
MESH = pl.DeviceIdType.MESH

STEP = 0.2
STRESS = ((0, 5, 4), (5, 1, 3), (4, 3, 2))
OFF = ((1, 2), (0, 2), (0, 1))
NF, NN, E, NW, ND = 9, 35, 256, 32, 128
OWN, TAB = 1024, 1152
ROWS = 27 * 16
MOVED = (*range(384, 399), *range(400, 409))


def tables():
    triangle = [(a, b) for a in range(5) for b in range(5 - a)]
    nodes = [(a, b, c) for a in range(5) for b in range(5 - a) for c in range(5 - a - b)]
    face = np.zeros((4, 15), np.int32)
    for at, (a, b) in enumerate(triangle):
        for f, key in enumerate(((a, b, 0), (a, 0, b), (0, a, b), (a, b, 4 - a - b))):
            face[f, at] = nodes.index(key)
    orders = [(0, 1, 2), (1, 2, 0), (2, 0, 1), (0, 2, 1), (2, 1, 0), (1, 0, 2)]
    turning = np.zeros((6, 15), np.int32)
    for o, order in enumerate(orders):
        for at, (a, b) in enumerate(triangle):
            triple = (a, b, 4 - a - b)
            turning[o, at] = triangle.index((triple[order[0]], triple[order[1]]))
    return face, turning


def constants():
    face, turning = tables()
    pick = np.zeros((128, 144), np.float32)
    for f in range(4):
        for m in range(15):
            pick[f * 16 + m, face[f, m]] = 1.0
            pick[64 + f * 16 + m, 48 + face[f, m]] = 1.0
    turn = np.full((16, 128), 15, np.int32)
    for o in range(6):
        turn[:15, o] = turning[o]
    return pick, turn


def split(x):
    hi = x.astype(bf16)
    lo = (x - hi.astype(f32)).astype(bf16)
    return hi, lo


def nn(a, b):
    return lax.dot_general(a, b, (((1,), (0,)), ((), ())), preferred_element_type=f32)


def nt(a, b):
    return lax.dot_general(a, b, (((1,), (1,)), ((), ())), preferred_element_type=f32)


def tn(a, b):
    return lax.dot_general(a, b, (((0,), (0,)), ((), ())), preferred_element_type=f32)


def iota(shape, dim, kind=i32):
    return lax.broadcasted_iota(kind, shape, dim)


def below(x, rows):
    return jnp.concatenate([x, jnp.zeros((rows - x.shape[0], x.shape[1]), x.dtype)], axis=0)


def lanes3(x, width):
    hi = x.astype(bf16).astype(f32)
    lo = x - hi
    zero = jnp.zeros((x.shape[0], width - x.shape[1]), f32)
    return jnp.concatenate([hi, zero, hi, zero, lo, zero], axis=1).astype(bf16)


def rows3(x):
    hi, lo = split(x)
    return jnp.concatenate([hi, lo, hi], axis=0)


N_OPS = 21


def kernel(*refs):
    sources, (out_d, out_a, out_h) = refs[:N_OPS], refs[N_OPS:N_OPS + 3]
    held = refs[N_OPS + 3:2 * N_OPS + 3]
    isem = refs[-1]
    loads = [pltpu.make_async_copy(a, b, isem.at[at]) for at, (a, b) in enumerate(zip(sources, held))]
    for load in loads:
        load.start()
    work(loads, *held, out_d, out_a, out_h, *refs[2 * N_OPS + 3:-1])


def work(
    loads,
    s0, dl, ad, model, geometry, normals, face_scale, derivative, lift, prolong, coarse, reg, observe,
    owner, local, child, neighbor, orient, send_face, pick, turn,
    out_d, out_a, out_h,
    tab, hot, dq, jump, hn, xl, fs, ltr, rst, c1,
    tr_s, tr_r, ag_s, ag_r, p1, p2, p3, chot, new_d, new_a, lmat, order, packed, left,
    ssem, rsem, osem,
):
    region, wave = lax.axis_index("region"), lax.axis_index("wave")
    me = region * NW + wave
    core = lax.rem(wave, 2)
    chip = lax.div(me, 2)
    barrier = pltpu.get_barrier_semaphore()

    def greet(there):
        pl.semaphore_signal(barrier, inc=1, device_id=there, device_id_type=MESH)

    def alike(i):
        d = lax.rem(me + 2 * i, ND)
        return lax.div(d, 2), (lax.div(d, NW), lax.rem(d, NW))

    def each(low, high, act):
        def one(i, c):
            act(i)
            return c

        lax.fori_loop(low, high, one, 0)

    sibling = (region, wave + 1 - 2 * core)
    each(0, 16, lambda i: greet((region, lax.rem(wave + 2 * i + 1, NW))))
    each(1, 64, lambda i: greet(alike(i)[1]))

    def send(src, dst, at, there):
        pltpu.make_async_remote_copy(
            src_ref=src, dst_ref=dst, send_sem=ssem.at[at], recv_sem=rsem.at[at], device_id=there, device_id_type=MESH
        ).start()

    def wait(part, sem):
        pltpu.make_async_copy(part, part, sem).wait()

    for load in loads:
        load.wait()

    cs = jnp.concatenate([coarse[...], jnp.zeros((2, 32), f32)], axis=0)
    cst = jnp.concatenate([cs, jnp.zeros((32, 96), f32)], axis=1).T
    ag_s[...] = jnp.concatenate([cst[q * 8:q * 8 + 8, 0:32] for q in range(4)], axis=1)
    ag_r[pl.ds(chip, 1), pl.ds(core, 1)] = ag_s[...].reshape(1, 1, 8, 128)

    u = (iota((ND, E), 0) == owner[...]).astype(f32).astype(bf16)
    ub = u.astype(f32)
    tri = (iota((E, E), 0) < iota((E, E), 1)).astype(f32).astype(bf16)
    before = jnp.sum(nn(u, tri) * ub, axis=0, keepdims=True).astype(i32)

    for k in range(3):
        c1[k * 40:(k + 1) * 40, :] = lanes3(below(derivative[k], 40), 48)
    c1[120:248, :] = pick[...]
    for s, ref in enumerate((s0, dl, ad)):
        for c in range(NF):
            sc = s * NF + c
            got = nn(c1[...], rows3(below(ref[c], 48)))
            dq[sc] = got[0:120]
            for f in range(4):
                span = slice(f * E, (f + 1) * E)
                tab[0, sc * 16:(sc + 1) * 16, span] = got[120 + f * 16:136 + f * 16].astype(bf16)
                tab[1, sc * 16:(sc + 1) * 16, span] = got[184 + f * 16:200 + f * 16].astype(bf16)

    turned = iota((8, 128), 1)
    turned = (turned & 31) * 4 + lax.shift_right_logical(turned, 5)
    chosen = jnp.broadcast_to(send_face[...].astype(f32), (8, 128))
    chosen = jnp.take_along_axis(chosen, turned, axis=1, mode="promise_in_bounds").astype(i32)
    pickt = (iota((OWN, 128), 0) == chosen[0:1]).astype(f32).astype(bf16)
    packed[...] = nn(tab[0, :, 0:OWN], pickt) + nn(tab[1, :, 0:OWN], pickt)
    for block, row in enumerate(MOVED):
        packed[block * 16 + 15:block * 16 + 16, :] = packed[row:row + 1, :]
    left[0:6, :] = packed[409:415, :]
    left[6:21, :] = packed[416:431, :]
    left[21:32, :] = jnp.zeros((11, 128), f32)
    rows_s = tr_s.reshape(13, NW, 128)
    for j in range(3):
        rows_s[j * 4:j * 4 + 4] = packed[j * 128:(j + 1) * 128, :].T.reshape(4, NW, 128)
    last = left[...].T
    rows_s[12] = jnp.concatenate([last[c * 32:(c + 1) * 32] for c in range(4)], axis=1)

    pl.semaphore_wait(barrier, 79)

    def send_trace(i):
        w = lax.rem(wave + i, NW)
        send(tr_s.at[:, pl.ds(w, 1)], tr_r.at[:, pl.ds(wave, 1)], 0, (region, w))

    each(1, NW, send_trace)
    each(1, 64, lambda i: send(ag_s, ag_r.at[chip, core], 1, alike(i)[1]))
    tr_r[:, pl.ds(wave, 1)] = tr_s[:, pl.ds(wave, 1)]

    for f in range(4):
        named = neighbor[f:f + 1, :]
        far = OWN + (named & 3) * 32 + lax.shift_right_logical(named - OWN, 2)
        row = jnp.where(named < OWN, named, far).astype(i16)
        hot[:, f * E:(f + 1) * E] = jnp.where(
            iota((TAB, E), 0, i16) == row, jnp.ones((), bf16), jnp.zeros((), bf16)
        )

    line = (owner[...] * 8 + (local[...] & 7)).astype(i16)
    chot[...] = jnp.where(iota((1024, E), 0, i16) == line, jnp.ones((), bf16), jnp.zeros((), bf16))

    for f in range(4):
        span = slice(f * E, (f + 1) * E)
        jump[:, span] = nn(tab[0, :, 0:OWN], hot[0:OWN, span]) + nn(tab[1, :, 0:OWN], hot[0:OWN, span])

    for f in range(4):
        span = slice(f * E, (f + 1) * E)
        h = 0.5 * face_scale[f:f + 1, :]
        for j in range(3):
            hn[j, :, span] = jnp.broadcast_to(h * normals[j, f:f + 1, :], (8, E))
        hn[3, :, span] = jnp.broadcast_to(h, (8, E))

    ltr[...] = jnp.zeros_like(ltr)
    for f in range(4):
        for m in range(15):
            ltr[f * 16 + m:f * 16 + m + 1, 0:NN] = lift[m, f:f + 1, :]
    lh, ll = split(ltr[...].T[0:40])
    lmat[...] = jnp.concatenate([lh.astype(f32), lh.astype(f32), ll.astype(f32)], axis=1).astype(bf16)

    for f in range(4):
        span = slice(f * E, (f + 1) * E)
        idx = jnp.full((16, E), 15, i32)
        for q in range(6):
            idx = jnp.where(orient[f:f + 1, :] == q, turn[:, q:q + 1], idx)
        order[:, span] = idx

    geo = [geometry[q:q + 1, :] for q in range(9)]

    def grad(sc, i):
        return sum(geo[3 * i + k] * dq[sc, k * 40:(k + 1) * 40, :] for k in range(3))

    for s in range(3):
        base = s * NF
        for i in range(3):
            fs[s, i] = sum(grad(base + 3 + STRESS[i][j], j) for j in range(3))
            fs[s, 3 + i] = grad(base + i, i)
        for at, (i, j) in enumerate(OFF):
            fs[s, 6 + at] = grad(base + j, i) + grad(base + i, j)

    mask = (iota((8, E), 0) == child[...]).astype(f32)
    pm = prolong[...].reshape(80, NN)
    pm40 = jnp.concatenate([pm, jnp.zeros((80, 5), f32)], axis=1)
    ph, pw = split(pm40)
    pm3 = jnp.concatenate([ph, ph, pw], axis=0)
    pm144 = lanes3(pm, 48)

    wait(tr_r.at[:, pl.ds(0, NW - 1)], rsem.at[0])
    rows_r = tr_r.reshape(13, NW, 128)
    for j in range(3):
        packed[j * 128:(j + 1) * 128, :] = rows_r[j * 4:j * 4 + 4].reshape(128, 128).T
    last = rows_r[12]
    left[...] = jnp.concatenate([last[:, c * 32:(c + 1) * 32] for c in range(4)], axis=0).T
    for row in (399, 415, 431):
        packed[row:row + 1, :] = jnp.zeros((1, 128), f32)
    for block, row in enumerate(MOVED):
        packed[row:row + 1, :] = packed[block * 16 + 15:block * 16 + 16, :]
    packed[409:415, :] = left[0:6, :]
    packed[416:431, :] = left[6:21, :]
    hi, lo = split(packed[...])
    tab[0, :, OWN:TAB] = hi
    tab[1, :, OWN:TAB] = lo
    for f in range(4):
        span = slice(f * E, (f + 1) * E)
        jump[:, span] += nn(tab[0, :, OWN:TAB], hot[OWN:TAB, span]) + nn(tab[1, :, OWN:TAB], hot[OWN:TAB, span])

    for f in range(4):
        span = slice(f * E, (f + 1) * E)
        idx = order[:, span]
        low = idx < 8
        idx = idx & 7
        ia, ib = idx[0:8], idx[8:16]
        for sc in range(27):
            a = jump[sc * 16:sc * 16 + 8, span]
            b = jump[sc * 16 + 8:sc * 16 + 16, span]
            own = tab[0, sc * 16:sc * 16 + 16, span].astype(f32) + tab[1, sc * 16:sc * 16 + 16, span].astype(f32)
            for t, ix in enumerate((ia, ib)):
                ga = jnp.take_along_axis(a, ix, axis=0, mode="promise_in_bounds")
                gb = jnp.take_along_axis(b, ix, axis=0, mode="promise_in_bounds")
                jump[sc * 16 + t * 8:sc * 16 + t * 8 + 8, span] = (
                    jnp.where(low[t * 8:t * 8 + 8], ga, gb) - own[t * 8:t * 8 + 8]
                )

    wait(ag_r.at[pl.ds(0, 63), 0], rsem.at[1])
    send(ag_r.at[:, pl.ds(core, 1)], ag_r.at[:, pl.ds(core, 1)], 2, sibling)

    def terms(s):
        for f in range(4):
            span = slice(f * E, (f + 1) * E)
            n = [jnp.concatenate([hn[j, :, span]] * 2, axis=0) for j in range(4)]
            q = [jump[(s * NF + c) * 16:(s * NF + c) * 16 + 16, span] for c in range(NF)]
            chans = [sum(n[j] * q[3 + STRESS[i][j]] for j in range(3)) for i in range(3)]
            chans += [n[j] * q[j] for j in range(3)]
            chans += [n[i] * q[j] + n[j] * q[i] for i, j in OFF]
            if s > 0:
                chans += [n[3] * q[c] for c in range(NF)]
            for at, g in enumerate(chans):
                hi, lo = split(g)
                xl[at, f * 16:f * 16 + 16, :] = hi
                xl[at, 64 + f * 16:80 + f * 16, :] = lo
                xl[at, 128 + f * 16:144 + f * 16, :] = hi
        for at in range(9):
            fs[s, at] += nn(lmat[...], xl[at])
        if s > 0:
            for at in range(9, 18):
                fs[s, at] = nn(lmat[...], xl[at])

    terms(0)

    terms(1)
    terms(2)

    wait(ag_r.at[:, pl.ds(0, 1)], rsem.at[2])
    chi, clo = split(ag_r[...].reshape(1024, 128).T)
    found = jnp.where(
        lax.div(iota((128, E), 0), 32) == lax.shift_right_logical(local[...], 3), nn(chi, chot[...]) + nn(clo, chot[...]), 0.0
    )
    found = found[0:32] + found[32:64] + found[64:96] + found[96:128]
    fine = []
    for p in range(3):
        z = jnp.concatenate([mask * found[p * 10 + k:p * 10 + k + 1, :] for k in range(10)], axis=0)
        fine.append(tn(pm3, rows3(z)))

    m0, m1, m2 = (below(model[p], 40) for p in range(3))

    def lam(s):
        return fs[s, 3] + fs[s, 4] + fs[s, 5]

    def mu(s, k):
        return 2.0 * fs[s, 3 + k] if k < 3 else fs[s, 3 + k]

    lam0 = lam(0)
    lam1 = m1 * lam(1) + fine[1] * lam0
    lam2 = m1 * lam(2)
    obs = below(observe[...], 40)
    gb = jnp.zeros((40, E), f32)
    tr = jnp.zeros((40, E), f32)
    gm = jnp.zeros((40, E), f32)
    for c in range(NF):
        if c < 3:
            wave_d = m0 * fs[1, c] + fine[0] * fs[0, c]
            wave_a = m0 * fs[2, c]
        else:
            wave_d = m2 * mu(1, c - 3) + fine[2] * mu(0, c - 3)
            wave_a = m2 * mu(2, c - 3)
            if c < 6:
                wave_d = wave_d + lam1
                wave_a = wave_a + lam2
        nd = below(dl[c], 40) + STEP * (wave_d + fs[1, 9 + c])
        na = below(ad[c], 40) + STEP * (wave_a + fs[2, 9 + c] + obs * nd)
        new_d[c] = nd[0:NN]
        new_a[c] = na[0:NN]
        if c < 3:
            gb = gb + na * fs[0, c]
        else:
            gm = gm + na * mu(0, c - 3)
            if c < 6:
                tr = tr + na
    stores = [pltpu.make_async_copy(new_d, out_d, osem.at[0]), pltpu.make_async_copy(new_a, out_a, osem.at[1])]
    for store in stores:
        store.start()
    fine_grad = (STEP * gb, STEP * tr * lam0, STEP * gm)

    rst[30:31, :] = local[...].astype(f32)
    rst[31:32, :] = jnp.zeros((1, E), f32)
    for p in range(3):
        r = nn(pm144, rows3(below(fine_grad[p], 48)))
        rst[p * 10:(p + 1) * 10, :] = jnp.sum(r.reshape(10, 8, E) * mask[None], axis=1)
    slot = lax.div(iota((128, E), 0), 32) == before
    wh, wl = split(jnp.where(slot, jnp.concatenate([rst[...]] * 4, axis=0), 0.0))
    p1.reshape(ND, 128)[...] = nt(u, wh) + nt(u, wl)
    send(p1.at[:, pl.ds(1 - core, 1)], p2.at[:, pl.ds(core, 1)], 3, sibling)
    p2[:, pl.ds(core, 1)] = p1[:, pl.ds(core, 1)]
    wait(p2.at[:, pl.ds(0, 1)], rsem.at[3])

    def send_partial(i):
        to, there = alike(i)
        send(p2.at[to], p3.at[chip], 4, there)

    each(1, 64, send_partial)
    p3[pl.ds(chip, 1)] = p2[pl.ds(chip, 1)]
    wait(p3.at[pl.ds(0, 63)], rsem.at[4])
    gh, gl = split(p3.reshape(ND, 128)[...])
    place_of = lax.rem(iota((128, 128), 1), 32)
    spread = (iota((128, 128), 0) == iota((128, 128), 1) - place_of + 30).astype(f32).astype(bf16)
    asked = (nn(gh, spread).astype(i32) == place_of).astype(f32).astype(bf16)
    same = lax.div(iota((128, 128), 0), 32) == lax.div(iota((128, 128), 1), 32)
    total = jnp.where(same, tn(gh, asked) + tn(gl, asked), 0.0)
    total = total[0:32] + total[32:64] + total[64:96] + total[96:128]
    total = total[:, 0:32] + total[:, 32:64] + total[:, 64:96] + total[:, 96:128]
    out_h[...] = total[0:30] + reg[...] * coarse[...]

    wait(tr_s.at[:, pl.ds(0, NW - 1)], ssem.at[0])
    wait(ag_r.at[pl.ds(0, 63), 0], ssem.at[1])
    wait(ag_r.at[:, pl.ds(0, 1)], ssem.at[2])
    wait(p1.at[:, pl.ds(0, 1)], ssem.at[3])
    wait(p2.at[pl.ds(0, 63)], ssem.at[4])
    for store in stores:
        store.wait()


def place(*refs):
    isem, osem = refs[-2:]
    loads = [pltpu.make_async_copy(refs[at], refs[6 + at], isem.at[at]) for at in range(3)]
    stores = [pltpu.make_async_copy(refs[6 + at], refs[3 + at], osem.at[at]) for at in range(3)]
    for load in loads:
        load.start()
    for load, store in zip(loads, stores):
        load.wait()
        store.start()
    for store in stores:
        store.wait()


def body(
    state0, delta, adjoint, model, geometry, normals, face_scale, derivative, lift, prolong, coarse_step, reg_weight,
    observe, owner, coarse_local, child, neighbor, orient, send_face,
):
    pick, turn = constants()
    ops = (
        state0, delta, adjoint, model, geometry, normals, face_scale, derivative,
        lift.transpose(2, 0, 1), prolong.transpose(2, 0, 1), coarse_step, reg_weight, observe,
        owner.reshape(1, E), coarse_local.reshape(1, E), child.reshape(1, E), neighbor, orient, send_face.reshape(1, 128),
        jnp.asarray(pick, bf16), jnp.asarray(turn),
    )
    vmem = pl.BlockSpec(memory_space=pltpu.VMEM)
    anywhere = pl.BlockSpec(memory_space=pl.ANY)
    hbm = pl.BlockSpec(memory_space=pltpu.HBM)
    row = pltpu.VMEM((64, 2, 1, 128), f32)
    results = (
        jax.ShapeDtypeStruct((NF, NN, E), f32),
        jax.ShapeDtypeStruct((NF, NN, E), f32),
        jax.ShapeDtypeStruct((30, 32), f32),
    )
    found = pl.pallas_call(
        kernel,
        out_shape=results,
        in_specs=[hbm] * len(ops),
        out_specs=(hbm, hbm, vmem),
        scratch_shapes=[
            *(pltpu.VMEM(op.shape, op.dtype) for op in ops),
            pltpu.VMEM((2, ROWS, TAB), bf16),
            pltpu.VMEM((TAB, OWN), bf16),
            pltpu.VMEM((27, 120, E), f32),
            pltpu.VMEM((ROWS, OWN), f32),
            pltpu.VMEM((4, 8, OWN), f32),
            pltpu.VMEM((18, 192, E), bf16),
            pltpu.VMEM((3, 18, 40, E), f32),
            pltpu.VMEM((64, 128), f32),
            pltpu.VMEM((32, E), f32),
            pltpu.VMEM((248, 144), bf16),
            pltpu.VMEM((13, NW, 1, 128), f32),
            pltpu.VMEM((13, NW, 1, 128), f32),
            pltpu.VMEM((8, 128), f32),
            pltpu.VMEM((64, 2, 8, 128), f32),
            row, row, row,
            pltpu.VMEM((1024, E), bf16),
            pltpu.VMEM((NF, NN, E), f32),
            pltpu.VMEM((NF, NN, E), f32),
            pltpu.VMEM((40, 192), bf16),
            pltpu.VMEM((16, OWN), i32),
            pltpu.VMEM((ROWS, 128), f32),
            pltpu.VMEM((32, 128), f32),
            pltpu.SemaphoreType.DMA((5,)),
            pltpu.SemaphoreType.DMA((5,)),
            pltpu.SemaphoreType.DMA((2,)),
            pltpu.SemaphoreType.DMA((N_OPS,)),
        ],
        compiler_params=pltpu.CompilerParams(
            collective_id=0, has_side_effects=True, vmem_limit_bytes=60 * 1024 * 1024
        ),
    )(*ops)
    return pl.pallas_call(
        place,
        out_shape=results,
        in_specs=[anywhere] * 3,
        out_specs=(hbm, hbm, hbm),
        scratch_shapes=[
            *(pltpu.VMEM(r.shape, r.dtype) for r in results),
            pltpu.SemaphoreType.DMA((3,)),
            pltpu.SemaphoreType.DMA((3,)),
        ],
        compiler_params=pltpu.CompilerParams(vmem_limit_bytes=60 * 1024 * 1024),
    )(*found)


def solution(mesh):
    both = ("region", "wave")
    placed = (
        P(None, None, both), P(None, None, both), P(None, None, both), P(None, None, both), P(None, both),
        P(None, None, both), P(None, both), P(), P(), P(), P(None, both), P(None, both), P(None, both),
        P(both, None), P(both), P(both), P(None, both), P(None, both), P(both),
    )
    return jax.shard_map(
        body, mesh=mesh, in_specs=placed,
        out_specs=(P(None, None, both), P(None, None, both), P(None, both)), check_vma=False,
    )
```

```python
import functools

import jax
import jax.numpy as jnp
import numpy as np
from jax import lax
from jax.experimental import pallas as pl
from jax.experimental.pallas import tpu as pltpu
from jax.sharding import PartitionSpec as P

f32, bf16, i32, i16 = jnp.float32, jnp.bfloat16, jnp.int32, jnp.int16
MESH = pl.DeviceIdType.MESH

STEP = 0.2
STRESS = ((0, 5, 4), (5, 1, 3), (4, 3, 2))
OFF = ((1, 2), (0, 2), (0, 1))
NF, NN, E, NW, ND = 9, 35, 256, 32, 128
OWN, TAB = 1024, 1152
ROWS = 27 * 16
MOVED = (*range(384, 399), *range(400, 409))


def tables():
    triangle = [(a, b) for a in range(5) for b in range(5 - a)]
    nodes = [(a, b, c) for a in range(5) for b in range(5 - a) for c in range(5 - a - b)]
    face = np.zeros((4, 15), np.int32)
    for at, (a, b) in enumerate(triangle):
        for f, key in enumerate(((a, b, 0), (a, 0, b), (0, a, b), (a, b, 4 - a - b))):
            face[f, at] = nodes.index(key)
    orders = [(0, 1, 2), (1, 2, 0), (2, 0, 1), (0, 2, 1), (2, 1, 0), (1, 0, 2)]
    turning = np.zeros((6, 15), np.int32)
    for o, order in enumerate(orders):
        for at, (a, b) in enumerate(triangle):
            triple = (a, b, 4 - a - b)
            turning[o, at] = triangle.index((triple[order[0]], triple[order[1]]))
    return face, turning


def constants():
    face, turning = tables()
    pick = np.zeros((128, 144), np.float32)
    for f in range(4):
        for m in range(15):
            pick[f * 16 + m, face[f, m]] = 1.0
            pick[64 + f * 16 + m, 48 + face[f, m]] = 1.0
    turn = np.full((16, 128), 15, np.int32)
    for o in range(6):
        turn[:15, o] = turning[o]
    return pick, turn


def split(x):
    hi = x.astype(bf16)
    lo = (x - hi.astype(f32)).astype(bf16)
    return hi, lo


def nn(a, b):
    return lax.dot_general(a, b, (((1,), (0,)), ((), ())), preferred_element_type=f32)


def nt(a, b):
    return lax.dot_general(a, b, (((1,), (1,)), ((), ())), preferred_element_type=f32)


def tn(a, b):
    return lax.dot_general(a, b, (((0,), (0,)), ((), ())), preferred_element_type=f32)


def iota(shape, dim, kind=i32):
    return lax.broadcasted_iota(kind, shape, dim)


def below(x, rows):
    return jnp.concatenate([x, jnp.zeros((rows - x.shape[0], x.shape[1]), x.dtype)], axis=0)


def lanes3(x, width):
    hi = x.astype(bf16).astype(f32)
    lo = x - hi
    zero = jnp.zeros((x.shape[0], width - x.shape[1]), f32)
    return jnp.concatenate([hi, zero, hi, zero, lo, zero], axis=1).astype(bf16)


def rows3(x):
    hi, lo = split(x)
    return jnp.concatenate([hi, lo, hi], axis=0)


N_OPS = 21


def kernel(*refs):
    sources, (out_d, out_a, out_h) = refs[:N_OPS], refs[N_OPS:N_OPS + 3]
    held = refs[N_OPS + 3:2 * N_OPS + 3]
    isem = refs[-1]
    loads = [pltpu.make_async_copy(a, b, isem.at[at]) for at, (a, b) in enumerate(zip(sources, held))]
    for load in loads:
        load.start()
    work(loads, *held, out_d, out_a, out_h, *refs[2 * N_OPS + 3:-1])


def work(
    loads,
    s0, dl, ad, model, geometry, normals, face_scale, derivative, lift, prolong, coarse, reg, observe,
    owner, local, child, neighbor, orient, send_face, pick, turn,
    out_d, out_a, out_h,
    tab, hot, dq, jump, hn, xl, fs, ltr, rst, c1,
    tr_s, tr_r, ag_s, ag_r, p1, p2, p3, chot, new_d, new_a, lmat, order, packed, left,
    ssem, rsem, osem,
):
    region, wave = lax.axis_index("region"), lax.axis_index("wave")
    me = region * NW + wave
    core = lax.rem(wave, 2)
    chip = lax.div(me, 2)
    barrier = pltpu.get_barrier_semaphore()

    def greet(there):
        pl.semaphore_signal(barrier, inc=1, device_id=there, device_id_type=MESH)

    def alike(i):
        d = lax.rem(me + 2 * i, ND)
        return lax.div(d, 2), (lax.div(d, NW), lax.rem(d, NW))

    def each(low, high, act):
        def one(i, c):
            act(i)
            return c

        lax.fori_loop(low, high, one, 0)

    half = lax.div(wave, 2)

    def level(i):
        return (region, lax.rem(wave + 2 * i, NW))

    def across(i):
        return (lax.rem(region + i, 4), wave)

    sibling = (region, wave + 1 - 2 * core)
    each(0, 16, lambda i: greet((region, lax.rem(wave + 2 * i + 1, NW))))
    each(1, 16, lambda i: greet(level(i)))
    each(1, 4, lambda i: greet(across(i)))

    def send(src, dst, at, there):
        pltpu.make_async_remote_copy(
            src_ref=src, dst_ref=dst, send_sem=ssem.at[at], recv_sem=rsem.at[at], device_id=there, device_id_type=MESH
        ).start()

    def wait(part, sem):
        pltpu.make_async_copy(part, part, sem).wait()

    for load in loads:
        load.wait()

    cs = jnp.concatenate([coarse[...], jnp.zeros((2, 32), f32)], axis=0)
    cst = jnp.concatenate([cs, jnp.zeros((32, 96), f32)], axis=1).T
    ag_s[...] = jnp.concatenate([cst[q * 8:q * 8 + 8, 0:32] for q in range(4)], axis=1)
    ag_r[pl.ds(half, 1), pl.ds(core, 1), pl.ds(region, 1)] = ag_s[...].reshape(1, 1, 1, 8, 128)

    u = (iota((ND, E), 0) == owner[...]).astype(f32).astype(bf16)
    ub = u.astype(f32)
    tri = (iota((E, E), 0) < iota((E, E), 1)).astype(f32).astype(bf16)
    before = jnp.sum(nn(u, tri) * ub, axis=0, keepdims=True).astype(i32)

    for k in range(3):
        c1[k * 40:(k + 1) * 40, :] = lanes3(below(derivative[k], 40), 48)
    c1[120:248, :] = pick[...]
    for s, ref in enumerate((s0, dl, ad)):
        for c in range(NF):
            sc = s * NF + c
            got = nn(c1[...], rows3(below(ref[c], 48)))
            dq[sc] = got[0:120]
            for f in range(4):
                span = slice(f * E, (f + 1) * E)
                tab[0, sc * 16:(sc + 1) * 16, span] = got[120 + f * 16:136 + f * 16].astype(bf16)
                tab[1, sc * 16:(sc + 1) * 16, span] = got[184 + f * 16:200 + f * 16].astype(bf16)

    turned = iota((8, 128), 1)
    turned = (turned & 31) * 4 + lax.shift_right_logical(turned, 5)
    chosen = jnp.broadcast_to(send_face[...].astype(f32), (8, 128))
    chosen = jnp.take_along_axis(chosen, turned, axis=1, mode="promise_in_bounds").astype(i32)
    pickt = (iota((OWN, 128), 0) == chosen[0:1]).astype(f32).astype(bf16)
    packed[...] = nn(tab[0, :, 0:OWN], pickt) + nn(tab[1, :, 0:OWN], pickt)
    for block, row in enumerate(MOVED):
        packed[block * 16 + 15:block * 16 + 16, :] = packed[row:row + 1, :]
    left[0:6, :] = packed[409:415, :]
    left[6:21, :] = packed[416:431, :]
    left[21:32, :] = jnp.zeros((11, 128), f32)
    rows_s = tr_s.reshape(13, NW, 128)
    for j in range(3):
        rows_s[j * 4:j * 4 + 4] = packed[j * 128:(j + 1) * 128, :].T.reshape(4, NW, 128)
    last = left[...].T
    rows_s[12] = jnp.concatenate([last[c * 32:(c + 1) * 32] for c in range(4)], axis=1)

    pl.semaphore_wait(barrier, 34)
    each(1, 4, lambda i: send(ag_s, ag_r.at[half, core, region], 1, across(i)))

    def send_trace(i):
        w = lax.rem(wave + i, NW)
        send(tr_s.at[:, pl.ds(w, 1)], tr_r.at[:, pl.ds(wave, 1)], 0, (region, w))

    each(1, NW, send_trace)
    tr_r[:, pl.ds(wave, 1)] = tr_s[:, pl.ds(wave, 1)]

    for f in range(4):
        named = neighbor[f:f + 1, :]
        far = OWN + (named & 3) * 32 + lax.shift_right_logical(named - OWN, 2)
        row = jnp.where(named < OWN, named, far).astype(i16)
        hot[:, f * E:(f + 1) * E] = jnp.where(
            iota((TAB, E), 0, i16) == row, jnp.ones((), bf16), jnp.zeros((), bf16)
        )

    wait(ag_r.at[0, 0, pl.ds(0, 3)], rsem.at[1])
    each(1, 16, lambda i: send(ag_r.at[half, core], ag_r.at[half, core], 5, level(i)))

    line = ((owner[...] & 31) * 4 + lax.shift_right_logical(owner[...], 5)) * 8
    line = (line + (local[...] & 7)).astype(i16)
    chot[...] = jnp.where(iota((1024, E), 0, i16) == line, jnp.ones((), bf16), jnp.zeros((), bf16))

    for f in range(4):
        span = slice(f * E, (f + 1) * E)
        jump[:, span] = nn(tab[0, :, 0:OWN], hot[0:OWN, span]) + nn(tab[1, :, 0:OWN], hot[0:OWN, span])

    for f in range(4):
        span = slice(f * E, (f + 1) * E)
        h = 0.5 * face_scale[f:f + 1, :]
        for j in range(3):
            hn[j, :, span] = jnp.broadcast_to(h * normals[j, f:f + 1, :], (8, E))
        hn[3, :, span] = jnp.broadcast_to(h, (8, E))

    ltr[...] = jnp.zeros_like(ltr)
    for f in range(4):
        for m in range(15):
            ltr[f * 16 + m:f * 16 + m + 1, 0:NN] = lift[m, f:f + 1, :]
    lh, ll = split(ltr[...].T[0:40])
    lmat[...] = jnp.concatenate([lh.astype(f32), lh.astype(f32), ll.astype(f32)], axis=1).astype(bf16)

    for f in range(4):
        span = slice(f * E, (f + 1) * E)
        idx = jnp.full((16, E), 15, i32)
        for q in range(6):
            idx = jnp.where(orient[f:f + 1, :] == q, turn[:, q:q + 1], idx)
        order[:, span] = idx

    geo = [geometry[q:q + 1, :] for q in range(9)]

    def grad(sc, i):
        return sum(geo[3 * i + k] * dq[sc, k * 40:(k + 1) * 40, :] for k in range(3))

    for s in range(3):
        base = s * NF
        for i in range(3):
            fs[s, i] = sum(grad(base + 3 + STRESS[i][j], j) for j in range(3))
            fs[s, 3 + i] = grad(base + i, i)
        for at, (i, j) in enumerate(OFF):
            fs[s, 6 + at] = grad(base + j, i) + grad(base + i, j)

    mask = (iota((8, E), 0) == child[...]).astype(f32)
    pm = prolong[...].reshape(80, NN)
    pm40 = jnp.concatenate([pm, jnp.zeros((80, 5), f32)], axis=1)
    ph, pw = split(pm40)
    pm3 = jnp.concatenate([ph, ph, pw], axis=0)
    pm144 = lanes3(pm, 48)

    wait(tr_r.at[:, pl.ds(0, NW - 1)], rsem.at[0])
    rows_r = tr_r.reshape(13, NW, 128)
    for j in range(3):
        packed[j * 128:(j + 1) * 128, :] = rows_r[j * 4:j * 4 + 4].reshape(128, 128).T
    last = rows_r[12]
    left[...] = jnp.concatenate([last[:, c * 32:(c + 1) * 32] for c in range(4)], axis=0).T
    for row in (399, 415, 431):
        packed[row:row + 1, :] = jnp.zeros((1, 128), f32)
    for block, row in enumerate(MOVED):
        packed[row:row + 1, :] = packed[block * 16 + 15:block * 16 + 16, :]
    packed[409:415, :] = left[0:6, :]
    packed[416:431, :] = left[6:21, :]
    hi, lo = split(packed[...])
    tab[0, :, OWN:TAB] = hi
    tab[1, :, OWN:TAB] = lo
    for f in range(4):
        span = slice(f * E, (f + 1) * E)
        jump[:, span] += nn(tab[0, :, OWN:TAB], hot[OWN:TAB, span]) + nn(tab[1, :, OWN:TAB], hot[OWN:TAB, span])

    for f in range(4):
        span = slice(f * E, (f + 1) * E)
        idx = order[:, span]
        low = idx < 8
        idx = idx & 7
        ia, ib = idx[0:8], idx[8:16]
        for sc in range(27):
            a = jump[sc * 16:sc * 16 + 8, span]
            b = jump[sc * 16 + 8:sc * 16 + 16, span]
            own = tab[0, sc * 16:sc * 16 + 16, span].astype(f32) + tab[1, sc * 16:sc * 16 + 16, span].astype(f32)
            for t, ix in enumerate((ia, ib)):
                ga = jnp.take_along_axis(a, ix, axis=0, mode="promise_in_bounds")
                gb = jnp.take_along_axis(b, ix, axis=0, mode="promise_in_bounds")
                jump[sc * 16 + t * 8:sc * 16 + t * 8 + 8, span] = (
                    jnp.where(low[t * 8:t * 8 + 8], ga, gb) - own[t * 8:t * 8 + 8]
                )

    wait(ag_r.at[pl.ds(0, 15), 0], rsem.at[5])
    send(ag_r.at[:, pl.ds(core, 1)], ag_r.at[:, pl.ds(core, 1)], 2, sibling)

    def terms(s):
        for f in range(4):
            span = slice(f * E, (f + 1) * E)
            n = [jnp.concatenate([hn[j, :, span]] * 2, axis=0) for j in range(4)]
            q = [jump[(s * NF + c) * 16:(s * NF + c) * 16 + 16, span] for c in range(NF)]
            chans = [sum(n[j] * q[3 + STRESS[i][j]] for j in range(3)) for i in range(3)]
            chans += [n[j] * q[j] for j in range(3)]
            chans += [n[i] * q[j] + n[j] * q[i] for i, j in OFF]
            if s > 0:
                chans += [n[3] * q[c] for c in range(NF)]
            for at, g in enumerate(chans):
                hi, lo = split(g)
                xl[at, f * 16:f * 16 + 16, :] = hi
                xl[at, 64 + f * 16:80 + f * 16, :] = lo
                xl[at, 128 + f * 16:144 + f * 16, :] = hi
        for at in range(9):
            fs[s, at] += nn(lmat[...], xl[at])
        if s > 0:
            for at in range(9, 18):
                fs[s, at] = nn(lmat[...], xl[at])

    terms(0)

    terms(1)
    terms(2)

    m0, m1, m2 = (below(model[p], 40) for p in range(3))

    def lam(s):
        return fs[s, 3] + fs[s, 4] + fs[s, 5]

    def mu(s, k):
        return 2.0 * fs[s, 3 + k] if k < 3 else fs[s, 3 + k]

    for s, ref in ((1, dl), (2, ad)):
        lams = m1 * lam(s)
        for c in range(NF):
            grown = m0 * fs[s, c] if c < 3 else m2 * mu(s, c - 3)
            if 3 <= c < 6:
                grown = grown + lams
            fs[s, 9 + c] = below(ref[c], 40) + STEP * (grown + fs[s, 9 + c])
    lam0 = lam(0)

    wait(ag_r.at[:, pl.ds(0, 1)], rsem.at[2])
    chi, clo = split(ag_r[...].reshape(1024, 128).T)
    found = jnp.where(
        lax.div(iota((128, E), 0), 32) == lax.shift_right_logical(local[...], 3), nn(chi, chot[...]) + nn(clo, chot[...]), 0.0
    )
    found = found[0:32] + found[32:64] + found[64:96] + found[96:128]
    fine = []
    for p in range(3):
        z = jnp.concatenate([mask * found[p * 10 + k:p * 10 + k + 1, :] for k in range(10)], axis=0)
        fine.append(tn(pm3, rows3(z)))

    obs = STEP * below(observe[...], 40)
    fine = [STEP * x for x in fine]
    lam1 = fine[1] * lam0
    gb = jnp.zeros((40, E), f32)
    tr = jnp.zeros((40, E), f32)
    gm = jnp.zeros((40, E), f32)
    for c in range(NF):
        if c < 3:
            term = fs[0, c]
            nd = fs[1, 9 + c] + fine[0] * term
        else:
            term = mu(0, c - 3)
            more = fine[2] * term
            if c < 6:
                more = more + lam1
            nd = fs[1, 9 + c] + more
        na = fs[2, 9 + c] + obs * nd
        new_d[c] = nd[0:NN]
        new_a[c] = na[0:NN]
        if c < 3:
            gb = gb + na * term
        else:
            gm = gm + na * term
            if c < 6:
                tr = tr + na
    stores = [pltpu.make_async_copy(new_d, out_d, osem.at[0]), pltpu.make_async_copy(new_a, out_a, osem.at[1])]
    for store in stores:
        store.start()
    fine_grad = (STEP * gb, STEP * tr * lam0, STEP * gm)

    rst[30:31, :] = local[...].astype(f32)
    rst[31:32, :] = jnp.zeros((1, E), f32)
    for p in range(3):
        r = nn(pm144, rows3(below(fine_grad[p], 48)))
        rst[p * 10:(p + 1) * 10, :] = jnp.sum(r.reshape(10, 8, E) * mask[None], axis=1)
    slot = lax.div(iota((128, E), 0), 32) == before
    wh, wl = split(jnp.where(slot, jnp.concatenate([rst[...]] * 4, axis=0), 0.0))
    p1.reshape(ND, 128)[...] = nt(u, wh) + nt(u, wl)
    send(p1.at[:, pl.ds(1 - core, 1)], p2.at[:, pl.ds(core, 1)], 3, sibling)
    p2[:, pl.ds(core, 1)] = p1[:, pl.ds(core, 1)]
    wait(p2.at[:, pl.ds(0, 1)], rsem.at[3])

    def send_partial(i):
        to, there = alike(i)
        send(p2.at[to], p3.at[chip], 4, there)

    each(1, 64, send_partial)
    p3[pl.ds(chip, 1)] = p2[pl.ds(chip, 1)]
    wait(p3.at[pl.ds(0, 63)], rsem.at[4])
    gh, gl = split(p3.reshape(ND, 128)[...])
    place_of = lax.rem(iota((128, 128), 1), 32)
    spread = (iota((128, 128), 0) == iota((128, 128), 1) - place_of + 30).astype(f32).astype(bf16)
    asked = (nn(gh, spread).astype(i32) == place_of).astype(f32).astype(bf16)
    same = lax.div(iota((128, 128), 0), 32) == lax.div(iota((128, 128), 1), 32)
    total = jnp.where(same, tn(gh, asked) + tn(gl, asked), 0.0)
    total = total[0:32] + total[32:64] + total[64:96] + total[96:128]
    total = total[:, 0:32] + total[:, 32:64] + total[:, 64:96] + total[:, 96:128]
    out_h[...] = total[0:30] + reg[...] * coarse[...]

    wait(tr_s.at[:, pl.ds(0, NW - 1)], ssem.at[0])
    wait(ag_r.at[0, 0, pl.ds(0, 3)], ssem.at[1])
    wait(ag_r.at[pl.ds(0, 15), 0], ssem.at[5])
    wait(ag_r.at[:, pl.ds(0, 1)], ssem.at[2])
    wait(p1.at[:, pl.ds(0, 1)], ssem.at[3])
    wait(p2.at[pl.ds(0, 63)], ssem.at[4])
    for store in stores:
        store.wait()


def place(*refs):
    isem, osem = refs[-2:]
    loads = [pltpu.make_async_copy(refs[at], refs[6 + at], isem.at[at]) for at in range(3)]
    stores = [pltpu.make_async_copy(refs[6 + at], refs[3 + at], osem.at[at]) for at in range(3)]
    for load in loads:
        load.start()
    for load, store in zip(loads, stores):
        load.wait()
        store.start()
    for store in stores:
        store.wait()


def body(
    state0, delta, adjoint, model, geometry, normals, face_scale, derivative, lift, prolong, coarse_step, reg_weight,
    observe, owner, coarse_local, child, neighbor, orient, send_face,
):
    pick, turn = constants()
    ops = (
        state0, delta, adjoint, model, geometry, normals, face_scale, derivative,
        lift.transpose(2, 0, 1), prolong.transpose(2, 0, 1), coarse_step, reg_weight, observe,
        owner.reshape(1, E), coarse_local.reshape(1, E), child.reshape(1, E), neighbor, orient, send_face.reshape(1, 128),
        jnp.asarray(pick, bf16), jnp.asarray(turn),
    )
    vmem = pl.BlockSpec(memory_space=pltpu.VMEM)
    anywhere = pl.BlockSpec(memory_space=pl.ANY)
    hbm = pl.BlockSpec(memory_space=pltpu.HBM)
    row = pltpu.VMEM((64, 2, 1, 128), f32)
    results = (
        jax.ShapeDtypeStruct((NF, NN, E), f32),
        jax.ShapeDtypeStruct((NF, NN, E), f32),
        jax.ShapeDtypeStruct((30, 32), f32),
    )
    found = pl.pallas_call(
        kernel,
        out_shape=results,
        in_specs=[hbm] * len(ops),
        out_specs=(hbm, hbm, vmem),
        scratch_shapes=[
            *(pltpu.VMEM(op.shape, op.dtype) for op in ops),
            pltpu.VMEM((2, ROWS, TAB), bf16),
            pltpu.VMEM((TAB, OWN), bf16),
            pltpu.VMEM((27, 120, E), f32),
            pltpu.VMEM((ROWS, OWN), f32),
            pltpu.VMEM((4, 8, OWN), f32),
            pltpu.VMEM((18, 192, E), bf16),
            pltpu.VMEM((3, 18, 40, E), f32),
            pltpu.VMEM((64, 128), f32),
            pltpu.VMEM((32, E), f32),
            pltpu.VMEM((248, 144), bf16),
            pltpu.VMEM((13, NW, 1, 128), f32),
            pltpu.VMEM((13, NW, 1, 128), f32),
            pltpu.VMEM((8, 128), f32),
            pltpu.VMEM((16, 2, 4, 8, 128), f32),
            row, row, row,
            pltpu.VMEM((1024, E), bf16),
            pltpu.VMEM((NF, NN, E), f32),
            pltpu.VMEM((NF, NN, E), f32),
            pltpu.VMEM((40, 192), bf16),
            pltpu.VMEM((16, OWN), i32),
            pltpu.VMEM((ROWS, 128), f32),
            pltpu.VMEM((32, 128), f32),
            pltpu.SemaphoreType.DMA((6,)),
            pltpu.SemaphoreType.DMA((6,)),
            pltpu.SemaphoreType.DMA((2,)),
            pltpu.SemaphoreType.DMA((N_OPS,)),
        ],
        compiler_params=pltpu.CompilerParams(
            collective_id=0, has_side_effects=True, vmem_limit_bytes=60 * 1024 * 1024
        ),
    )(*ops)
    return pl.pallas_call(
        place,
        out_shape=results,
        in_specs=[anywhere] * 3,
        out_specs=(hbm, hbm, hbm),
        scratch_shapes=[
            *(pltpu.VMEM(r.shape, r.dtype) for r in results),
            pltpu.SemaphoreType.DMA((3,)),
            pltpu.SemaphoreType.DMA((3,)),
        ],
        compiler_params=pltpu.CompilerParams(vmem_limit_bytes=60 * 1024 * 1024),
    )(*found)


def solution(mesh):
    both = ("region", "wave")
    placed = (
        P(None, None, both), P(None, None, both), P(None, None, both), P(None, None, both), P(None, both),
        P(None, None, both), P(None, both), P(), P(), P(), P(None, both), P(None, both), P(None, both),
        P(both, None), P(both), P(both), P(None, both), P(None, both), P(both),
    )
    return jax.shard_map(
        body, mesh=mesh, in_specs=placed,
        out_specs=(P(None, None, both), P(None, None, both), P(None, both)), check_vma=False,
    )
```

```python
import functools

import jax
import jax.numpy as jnp
import numpy as np
from jax import lax
from jax.experimental import pallas as pl
from jax.experimental.pallas import tpu as pltpu
from jax.sharding import PartitionSpec as P

f32, bf16, i32, i16 = jnp.float32, jnp.bfloat16, jnp.int32, jnp.int16
MESH = pl.DeviceIdType.MESH

STEP = 0.2
STRESS = ((0, 5, 4), (5, 1, 3), (4, 3, 2))
OFF = ((1, 2), (0, 2), (0, 1))
NF, NN, E, NW, ND = 9, 35, 256, 32, 128
OWN, TAB = 1024, 1152
ROWS = 27 * 16
MOVED = (*range(384, 399), *range(400, 409))


def tables():
    triangle = [(a, b) for a in range(5) for b in range(5 - a)]
    nodes = [(a, b, c) for a in range(5) for b in range(5 - a) for c in range(5 - a - b)]
    face = np.zeros((4, 15), np.int32)
    for at, (a, b) in enumerate(triangle):
        for f, key in enumerate(((a, b, 0), (a, 0, b), (0, a, b), (a, b, 4 - a - b))):
            face[f, at] = nodes.index(key)
    orders = [(0, 1, 2), (1, 2, 0), (2, 0, 1), (0, 2, 1), (2, 1, 0), (1, 0, 2)]
    turning = np.zeros((6, 15), np.int32)
    for o, order in enumerate(orders):
        for at, (a, b) in enumerate(triangle):
            triple = (a, b, 4 - a - b)
            turning[o, at] = triangle.index((triple[order[0]], triple[order[1]]))
    return face, turning


def constants():
    face, turning = tables()
    pick = np.zeros((128, 144), np.float32)
    for f in range(4):
        for m in range(15):
            pick[f * 16 + m, face[f, m]] = 1.0
            pick[64 + f * 16 + m, 48 + face[f, m]] = 1.0
    turn = np.full((16, 128), 15, np.int32)
    for o in range(6):
        turn[:15, o] = turning[o]
    return pick, turn


def split(x):
    hi = x.astype(bf16)
    lo = (x - hi.astype(f32)).astype(bf16)
    return hi, lo


def nn(a, b):
    return lax.dot_general(a, b, (((1,), (0,)), ((), ())), preferred_element_type=f32)


def nt(a, b):
    return lax.dot_general(a, b, (((1,), (1,)), ((), ())), preferred_element_type=f32)


def tn(a, b):
    return lax.dot_general(a, b, (((0,), (0,)), ((), ())), preferred_element_type=f32)


def iota(shape, dim, kind=i32):
    return lax.broadcasted_iota(kind, shape, dim)


def below(x, rows):
    return jnp.concatenate([x, jnp.zeros((rows - x.shape[0], x.shape[1]), x.dtype)], axis=0)


def lanes3(x, width):
    hi = x.astype(bf16).astype(f32)
    lo = x - hi
    zero = jnp.zeros((x.shape[0], width - x.shape[1]), f32)
    return jnp.concatenate([hi, zero, hi, zero, lo, zero], axis=1).astype(bf16)


def rows3(x):
    hi, lo = split(x)
    return jnp.concatenate([hi, lo, hi], axis=0)


N_OPS = 21


def kernel(*refs):
    sources, (out_d, out_a, out_h) = refs[:N_OPS], refs[N_OPS:N_OPS + 3]
    held = refs[N_OPS + 3:2 * N_OPS + 3]
    isem = refs[-1]
    loads = [pltpu.make_async_copy(a, b, isem.at[at]) for at, (a, b) in enumerate(zip(sources, held))]
    for load in loads:
        load.start()
    work(loads, *held, out_d, out_a, out_h, *refs[2 * N_OPS + 3:-1])


def work(
    loads,
    s0, dl, ad, model, geometry, normals, face_scale, derivative, lift, prolong, coarse, reg, observe,
    owner, local, child, neighbor, orient, send_face, pick, turn,
    out_d, out_a, out_h,
    tab, hot, dq, jump, hn, xl, fs, ltr, rst, c1,
    tr_s, tr_r, ag_s, ag_r, p1, p3, chot, new_d, new_a, lmat, order, packed, left,
    ssem, rsem, osem,
):
    region, wave = lax.axis_index("region"), lax.axis_index("wave")
    me = region * NW + wave
    core = lax.rem(wave, 2)
    barrier = pltpu.get_barrier_semaphore()

    def greet(there):
        pl.semaphore_signal(barrier, inc=1, device_id=there, device_id_type=MESH)

    def each(low, high, act):
        def one(i, c):
            act(i)
            return c

        lax.fori_loop(low, high, one, 0)

    half = lax.div(wave, 2)

    def level(i):
        return (region, lax.rem(wave + 2 * i, NW))

    def across(i):
        return (lax.rem(region + i, 4), wave)

    sibling = (region, wave + 1 - 2 * core)
    each(0, 16, lambda i: greet((region, lax.rem(wave + 2 * i + 1, NW))))
    each(1, 16, lambda i: greet(level(i)))
    each(1, 4, lambda i: greet(across(i)))

    def send(src, dst, at, there):
        pltpu.make_async_remote_copy(
            src_ref=src, dst_ref=dst, send_sem=ssem.at[at], recv_sem=rsem.at[at], device_id=there, device_id_type=MESH
        ).start()

    def wait(part, sem):
        pltpu.make_async_copy(part, part, sem).wait()

    for load in loads:
        load.wait()

    cs = jnp.concatenate([coarse[...], jnp.zeros((2, 32), f32)], axis=0)
    cst = jnp.concatenate([cs, jnp.zeros((32, 96), f32)], axis=1).T
    ag_s[...] = jnp.concatenate([cst[q * 8:q * 8 + 8, 0:32] for q in range(4)], axis=1)
    ag_r[pl.ds(half, 1), pl.ds(core, 1), pl.ds(region, 1)] = ag_s[...].reshape(1, 1, 1, 8, 128)

    u = (iota((ND, E), 0) == owner[...]).astype(f32).astype(bf16)
    ub = u.astype(f32)
    tri = (iota((E, E), 0) < iota((E, E), 1)).astype(f32).astype(bf16)
    before = jnp.sum(nn(u, tri) * ub, axis=0, keepdims=True).astype(i32)

    for k in range(3):
        c1[k * 40:(k + 1) * 40, :] = lanes3(below(derivative[k], 40), 48)
    c1[120:248, :] = pick[...]
    for s, ref in enumerate((s0, dl, ad)):
        for c in range(NF):
            sc = s * NF + c
            got = nn(c1[...], rows3(below(ref[c], 48)))
            dq[sc] = got[0:120]
            for f in range(4):
                span = slice(f * E, (f + 1) * E)
                tab[0, sc * 16:(sc + 1) * 16, span] = got[120 + f * 16:136 + f * 16].astype(bf16)
                tab[1, sc * 16:(sc + 1) * 16, span] = got[184 + f * 16:200 + f * 16].astype(bf16)

    turned = iota((8, 128), 1)
    turned = (turned & 31) * 4 + lax.shift_right_logical(turned, 5)
    chosen = jnp.broadcast_to(send_face[...].astype(f32), (8, 128))
    chosen = jnp.take_along_axis(chosen, turned, axis=1, mode="promise_in_bounds").astype(i32)
    pickt = (iota((OWN, 128), 0) == chosen[0:1]).astype(f32).astype(bf16)
    packed[...] = nn(tab[0, :, 0:OWN], pickt) + nn(tab[1, :, 0:OWN], pickt)
    for block, row in enumerate(MOVED):
        packed[block * 16 + 15:block * 16 + 16, :] = packed[row:row + 1, :]
    left[0:6, :] = packed[409:415, :]
    left[6:21, :] = packed[416:431, :]
    left[21:32, :] = jnp.zeros((11, 128), f32)
    rows_s = tr_s.reshape(13, NW, 128)
    for j in range(3):
        rows_s[j * 4:j * 4 + 4] = packed[j * 128:(j + 1) * 128, :].T.reshape(4, NW, 128)
    last = left[...].T
    rows_s[12] = jnp.concatenate([last[c * 32:(c + 1) * 32] for c in range(4)], axis=1)

    pl.semaphore_wait(barrier, 34)
    each(1, 4, lambda i: send(ag_s, ag_r.at[half, core, region], 1, across(i)))

    def send_trace(i):
        w = lax.rem(wave + i, NW)
        send(tr_s.at[:, pl.ds(w, 1)], tr_r.at[:, pl.ds(wave, 1)], 0, (region, w))

    each(1, NW, send_trace)
    tr_r[:, pl.ds(wave, 1)] = tr_s[:, pl.ds(wave, 1)]

    for f in range(4):
        named = neighbor[f:f + 1, :]
        far = OWN + (named & 3) * 32 + lax.shift_right_logical(named - OWN, 2)
        row = jnp.where(named < OWN, named, far).astype(i16)
        hot[:, f * E:(f + 1) * E] = jnp.where(
            iota((TAB, E), 0, i16) == row, jnp.ones((), bf16), jnp.zeros((), bf16)
        )

    wait(ag_r.at[0, 0, pl.ds(0, 3)], rsem.at[1])
    each(1, 16, lambda i: send(ag_r.at[half, core], ag_r.at[half, core], 4, level(i)))

    line = ((owner[...] & 31) * 4 + lax.shift_right_logical(owner[...], 5)) * 8
    line = (line + (local[...] & 7)).astype(i16)
    chot[...] = jnp.where(iota((1024, E), 0, i16) == line, jnp.ones((), bf16), jnp.zeros((), bf16))

    for f in range(4):
        span = slice(f * E, (f + 1) * E)
        jump[:, span] = nn(tab[0, :, 0:OWN], hot[0:OWN, span]) + nn(tab[1, :, 0:OWN], hot[0:OWN, span])

    for f in range(4):
        span = slice(f * E, (f + 1) * E)
        h = 0.5 * face_scale[f:f + 1, :]
        for j in range(3):
            hn[j, :, span] = jnp.broadcast_to(h * normals[j, f:f + 1, :], (8, E))
        hn[3, :, span] = jnp.broadcast_to(h, (8, E))

    ltr[...] = jnp.zeros_like(ltr)
    for f in range(4):
        for m in range(15):
            ltr[f * 16 + m:f * 16 + m + 1, 0:NN] = lift[m, f:f + 1, :]
    lh, ll = split(ltr[...].T[0:40])
    lmat[...] = jnp.concatenate([lh.astype(f32), lh.astype(f32), ll.astype(f32)], axis=1).astype(bf16)

    for f in range(4):
        span = slice(f * E, (f + 1) * E)
        idx = jnp.full((16, E), 15, i32)
        for q in range(6):
            idx = jnp.where(orient[f:f + 1, :] == q, turn[:, q:q + 1], idx)
        order[:, span] = idx

    geo = [geometry[q:q + 1, :] for q in range(9)]

    def grad(sc, i):
        return sum(geo[3 * i + k] * dq[sc, k * 40:(k + 1) * 40, :] for k in range(3))

    for s in range(3):
        base = s * NF
        for i in range(3):
            fs[s, i] = sum(grad(base + 3 + STRESS[i][j], j) for j in range(3))
            fs[s, 3 + i] = grad(base + i, i)
        for at, (i, j) in enumerate(OFF):
            fs[s, 6 + at] = grad(base + j, i) + grad(base + i, j)

    mask = (iota((8, E), 0) == child[...]).astype(f32)
    pm = prolong[...].reshape(80, NN)
    pm40 = jnp.concatenate([pm, jnp.zeros((80, 5), f32)], axis=1)
    ph, pw = split(pm40)
    pm3 = jnp.concatenate([ph, ph, pw], axis=0)
    pm144 = lanes3(pm, 48)

    wait(tr_r.at[:, pl.ds(0, NW - 1)], rsem.at[0])
    rows_r = tr_r.reshape(13, NW, 128)
    for j in range(3):
        packed[j * 128:(j + 1) * 128, :] = rows_r[j * 4:j * 4 + 4].reshape(128, 128).T
    last = rows_r[12]
    left[...] = jnp.concatenate([last[:, c * 32:(c + 1) * 32] for c in range(4)], axis=0).T
    for row in (399, 415, 431):
        packed[row:row + 1, :] = jnp.zeros((1, 128), f32)
    for block, row in enumerate(MOVED):
        packed[row:row + 1, :] = packed[block * 16 + 15:block * 16 + 16, :]
    packed[409:415, :] = left[0:6, :]
    packed[416:431, :] = left[6:21, :]
    hi, lo = split(packed[...])
    tab[0, :, OWN:TAB] = hi
    tab[1, :, OWN:TAB] = lo
    for f in range(4):
        span = slice(f * E, (f + 1) * E)
        jump[:, span] += nn(tab[0, :, OWN:TAB], hot[OWN:TAB, span]) + nn(tab[1, :, OWN:TAB], hot[OWN:TAB, span])

    for f in range(4):
        span = slice(f * E, (f + 1) * E)
        idx = order[:, span]
        low = idx < 8
        idx = idx & 7
        ia, ib = idx[0:8], idx[8:16]
        for sc in range(27):
            a = jump[sc * 16:sc * 16 + 8, span]
            b = jump[sc * 16 + 8:sc * 16 + 16, span]
            own = tab[0, sc * 16:sc * 16 + 16, span].astype(f32) + tab[1, sc * 16:sc * 16 + 16, span].astype(f32)
            for t, ix in enumerate((ia, ib)):
                ga = jnp.take_along_axis(a, ix, axis=0, mode="promise_in_bounds")
                gb = jnp.take_along_axis(b, ix, axis=0, mode="promise_in_bounds")
                jump[sc * 16 + t * 8:sc * 16 + t * 8 + 8, span] = (
                    jnp.where(low[t * 8:t * 8 + 8], ga, gb) - own[t * 8:t * 8 + 8]
                )

    def terms(s):
        for f in range(4):
            span = slice(f * E, (f + 1) * E)
            n = [jnp.concatenate([hn[j, :, span]] * 2, axis=0) for j in range(4)]
            q = [jump[(s * NF + c) * 16:(s * NF + c) * 16 + 16, span] for c in range(NF)]
            chans = [sum(n[j] * q[3 + STRESS[i][j]] for j in range(3)) for i in range(3)]
            chans += [n[j] * q[j] for j in range(3)]
            chans += [n[i] * q[j] + n[j] * q[i] for i, j in OFF]
            if s > 0:
                chans += [n[3] * q[c] for c in range(NF)]
            for at, g in enumerate(chans):
                hi, lo = split(g)
                xl[at, f * 16:f * 16 + 16, :] = hi
                xl[at, 64 + f * 16:80 + f * 16, :] = lo
                xl[at, 128 + f * 16:144 + f * 16, :] = hi
        for at in range(9):
            fs[s, at] += nn(lmat[...], xl[at])
        if s > 0:
            for at in range(9, 18):
                fs[s, at] = nn(lmat[...], xl[at])

    terms(0)

    wait(ag_r.at[pl.ds(0, 15), 0], rsem.at[4])
    send(ag_r.at[:, pl.ds(core, 1)], ag_r.at[:, pl.ds(core, 1)], 2, sibling)

    terms(1)
    terms(2)

    m0, m1, m2 = (below(model[p], 40) for p in range(3))

    def lam(s):
        return fs[s, 3] + fs[s, 4] + fs[s, 5]

    def mu(s, k):
        return 2.0 * fs[s, 3 + k] if k < 3 else fs[s, 3 + k]

    for s, ref in ((1, dl), (2, ad)):
        lams = m1 * lam(s)
        for c in range(NF):
            grown = m0 * fs[s, c] if c < 3 else m2 * mu(s, c - 3)
            if 3 <= c < 6:
                grown = grown + lams
            fs[s, 9 + c] = below(ref[c], 40) + STEP * (grown + fs[s, 9 + c])
    lam0 = lam(0)

    wait(ag_r.at[:, pl.ds(0, 1)], rsem.at[2])
    chi, clo = split(ag_r[...].reshape(1024, 128).T)
    found = jnp.where(
        lax.div(iota((128, E), 0), 32) == lax.shift_right_logical(local[...], 3), nn(chi, chot[...]) + nn(clo, chot[...]), 0.0
    )
    found = found[0:32] + found[32:64] + found[64:96] + found[96:128]
    fine = []
    for p in range(3):
        z = jnp.concatenate([mask * found[p * 10 + k:p * 10 + k + 1, :] for k in range(10)], axis=0)
        fine.append(tn(pm3, rows3(z)))

    obs = STEP * below(observe[...], 40)
    fine = [STEP * x for x in fine]
    lam1 = fine[1] * lam0
    gb = jnp.zeros((40, E), f32)
    tr = jnp.zeros((40, E), f32)
    gm = jnp.zeros((40, E), f32)
    for c in range(NF):
        if c < 3:
            term = fs[0, c]
            nd = fs[1, 9 + c] + fine[0] * term
        else:
            term = mu(0, c - 3)
            more = fine[2] * term
            if c < 6:
                more = more + lam1
            nd = fs[1, 9 + c] + more
        na = fs[2, 9 + c] + obs * nd
        new_d[c] = nd[0:NN]
        new_a[c] = na[0:NN]
        if c < 3:
            gb = gb + na * term
        else:
            gm = gm + na * term
            if c < 6:
                tr = tr + na
    stores = [pltpu.make_async_copy(new_d, out_d, osem.at[0]), pltpu.make_async_copy(new_a, out_a, osem.at[1])]
    for store in stores:
        store.start()
    fine_grad = (STEP * gb, STEP * tr * lam0, STEP * gm)

    rst[30:31, :] = local[...].astype(f32)
    rst[31:32, :] = jnp.zeros((1, E), f32)
    for p in range(3):
        r = nn(pm144, rows3(below(fine_grad[p], 48)))
        rst[p * 10:(p + 1) * 10, :] = jnp.sum(r.reshape(10, 8, E) * mask[None], axis=1)
    slot = lax.div(iota((128, E), 0), 32) == before
    wh, wl = split(jnp.where(slot, jnp.concatenate([rst[...]] * 4, axis=0), 0.0))
    p1.reshape(ND, 128)[...] = nt(u, wh) + nt(u, wl)

    def send_partial(i):
        d = lax.rem(me + i, ND)
        send(p1.at[d], p3.at[me], 3, (lax.div(d, NW), lax.rem(d, NW)))

    each(1, ND, send_partial)
    p3[pl.ds(me, 1)] = p1[pl.ds(me, 1)]
    wait(p3.at[pl.ds(0, ND - 1)], rsem.at[3])
    gh, gl = split(p3.reshape(ND, 128)[...])
    place_of = lax.rem(iota((128, 128), 1), 32)
    spread = (iota((128, 128), 0) == iota((128, 128), 1) - place_of + 30).astype(f32).astype(bf16)
    asked = (nn(gh, spread).astype(i32) == place_of).astype(f32).astype(bf16)
    same = lax.div(iota((128, 128), 0), 32) == lax.div(iota((128, 128), 1), 32)
    total = jnp.where(same, tn(gh, asked) + tn(gl, asked), 0.0)
    total = total[0:32] + total[32:64] + total[64:96] + total[96:128]
    total = total[:, 0:32] + total[:, 32:64] + total[:, 64:96] + total[:, 96:128]
    out_h[...] = total[0:30] + reg[...] * coarse[...]

    wait(tr_s.at[:, pl.ds(0, NW - 1)], ssem.at[0])
    wait(ag_r.at[0, 0, pl.ds(0, 3)], ssem.at[1])
    wait(ag_r.at[pl.ds(0, 15), 0], ssem.at[4])
    wait(ag_r.at[:, pl.ds(0, 1)], ssem.at[2])
    wait(p1.at[pl.ds(0, ND - 1)], ssem.at[3])
    for store in stores:
        store.wait()


def place(*refs):
    isem, osem = refs[-2:]
    loads = [pltpu.make_async_copy(refs[at], refs[6 + at], isem.at[at]) for at in range(3)]
    stores = [pltpu.make_async_copy(refs[6 + at], refs[3 + at], osem.at[at]) for at in range(3)]
    for load in loads:
        load.start()
    for load, store in zip(loads, stores):
        load.wait()
        store.start()
    for store in stores:
        store.wait()


def body(
    state0, delta, adjoint, model, geometry, normals, face_scale, derivative, lift, prolong, coarse_step, reg_weight,
    observe, owner, coarse_local, child, neighbor, orient, send_face,
):
    pick, turn = constants()
    ops = (
        state0, delta, adjoint, model, geometry, normals, face_scale, derivative,
        lift.transpose(2, 0, 1), prolong.transpose(2, 0, 1), coarse_step, reg_weight, observe,
        owner.reshape(1, E), coarse_local.reshape(1, E), child.reshape(1, E), neighbor, orient, send_face.reshape(1, 128),
        jnp.asarray(pick, bf16), jnp.asarray(turn),
    )
    vmem = pl.BlockSpec(memory_space=pltpu.VMEM)
    anywhere = pl.BlockSpec(memory_space=pl.ANY)
    hbm = pl.BlockSpec(memory_space=pltpu.HBM)
    row = pltpu.VMEM((ND, 1, 128), f32)
    results = (
        jax.ShapeDtypeStruct((NF, NN, E), f32),
        jax.ShapeDtypeStruct((NF, NN, E), f32),
        jax.ShapeDtypeStruct((30, 32), f32),
    )
    found = pl.pallas_call(
        kernel,
        out_shape=results,
        in_specs=[hbm] * len(ops),
        out_specs=(hbm, hbm, vmem),
        scratch_shapes=[
            *(pltpu.VMEM(op.shape, op.dtype) for op in ops),
            pltpu.VMEM((2, ROWS, TAB), bf16),
            pltpu.VMEM((TAB, OWN), bf16),
            pltpu.VMEM((27, 120, E), f32),
            pltpu.VMEM((ROWS, OWN), f32),
            pltpu.VMEM((4, 8, OWN), f32),
            pltpu.VMEM((18, 192, E), bf16),
            pltpu.VMEM((3, 18, 40, E), f32),
            pltpu.VMEM((64, 128), f32),
            pltpu.VMEM((32, E), f32),
            pltpu.VMEM((248, 144), bf16),
            pltpu.VMEM((13, NW, 1, 128), f32),
            pltpu.VMEM((13, NW, 1, 128), f32),
            pltpu.VMEM((8, 128), f32),
            pltpu.VMEM((16, 2, 4, 8, 128), f32),
            row, row,
            pltpu.VMEM((1024, E), bf16),
            pltpu.VMEM((NF, NN, E), f32),
            pltpu.VMEM((NF, NN, E), f32),
            pltpu.VMEM((40, 192), bf16),
            pltpu.VMEM((16, OWN), i32),
            pltpu.VMEM((ROWS, 128), f32),
            pltpu.VMEM((32, 128), f32),
            pltpu.SemaphoreType.DMA((5,)),
            pltpu.SemaphoreType.DMA((5,)),
            pltpu.SemaphoreType.DMA((2,)),
            pltpu.SemaphoreType.DMA((N_OPS,)),
        ],
        compiler_params=pltpu.CompilerParams(
            collective_id=0, has_side_effects=True, vmem_limit_bytes=60 * 1024 * 1024
        ),
    )(*ops)
    return pl.pallas_call(
        place,
        out_shape=results,
        in_specs=[anywhere] * 3,
        out_specs=(hbm, hbm, hbm),
        scratch_shapes=[
            *(pltpu.VMEM(r.shape, r.dtype) for r in results),
            pltpu.SemaphoreType.DMA((3,)),
            pltpu.SemaphoreType.DMA((3,)),
        ],
        compiler_params=pltpu.CompilerParams(vmem_limit_bytes=60 * 1024 * 1024),
    )(*found)


def solution(mesh):
    both = ("region", "wave")
    placed = (
        P(None, None, both), P(None, None, both), P(None, None, both), P(None, None, both), P(None, both),
        P(None, None, both), P(None, both), P(), P(), P(), P(None, both), P(None, both), P(None, both),
        P(both, None), P(both), P(both), P(None, both), P(None, both), P(both),
    )
    return jax.shard_map(
        body, mesh=mesh, in_specs=placed,
        out_specs=(P(None, None, both), P(None, None, both), P(None, both)), check_vma=False,
    )
```

```python
import functools

import jax
import jax.numpy as jnp
import numpy as np
from jax import lax
from jax.experimental import pallas as pl
from jax.experimental.pallas import tpu as pltpu
from jax.sharding import PartitionSpec as P

f32, bf16, i32, i16 = jnp.float32, jnp.bfloat16, jnp.int32, jnp.int16
MESH = pl.DeviceIdType.MESH

STEP = 0.2
STRESS = ((0, 5, 4), (5, 1, 3), (4, 3, 2))
OFF = ((1, 2), (0, 2), (0, 1))
NF, NN, E, NW, ND = 9, 35, 256, 32, 128
OWN, TAB = 1024, 1152
ROWS = 27 * 16
MOVED = (*range(384, 399), *range(400, 409))


def tables():
    triangle = [(a, b) for a in range(5) for b in range(5 - a)]
    nodes = [(a, b, c) for a in range(5) for b in range(5 - a) for c in range(5 - a - b)]
    face = np.zeros((4, 15), np.int32)
    for at, (a, b) in enumerate(triangle):
        for f, key in enumerate(((a, b, 0), (a, 0, b), (0, a, b), (a, b, 4 - a - b))):
            face[f, at] = nodes.index(key)
    orders = [(0, 1, 2), (1, 2, 0), (2, 0, 1), (0, 2, 1), (2, 1, 0), (1, 0, 2)]
    turning = np.zeros((6, 15), np.int32)
    for o, order in enumerate(orders):
        for at, (a, b) in enumerate(triangle):
            triple = (a, b, 4 - a - b)
            turning[o, at] = triangle.index((triple[order[0]], triple[order[1]]))
    return face, turning


def constants():
    face, turning = tables()
    pick = np.zeros((128, 144), np.float32)
    for f in range(4):
        for m in range(15):
            pick[f * 16 + m, face[f, m]] = 1.0
            pick[64 + f * 16 + m, 48 + face[f, m]] = 1.0
    turn = np.full((16, 128), 15, np.int32)
    for o in range(6):
        turn[:15, o] = turning[o]
    return pick, turn


def split(x):
    hi = x.astype(bf16)
    lo = (x - hi.astype(f32)).astype(bf16)
    return hi, lo


def nn(a, b):
    return lax.dot_general(a, b, (((1,), (0,)), ((), ())), preferred_element_type=f32)


def nt(a, b):
    return lax.dot_general(a, b, (((1,), (1,)), ((), ())), preferred_element_type=f32)


def tn(a, b):
    return lax.dot_general(a, b, (((0,), (0,)), ((), ())), preferred_element_type=f32)


def iota(shape, dim, kind=i32):
    return lax.broadcasted_iota(kind, shape, dim)


def below(x, rows):
    return jnp.concatenate([x, jnp.zeros((rows - x.shape[0], x.shape[1]), x.dtype)], axis=0)


def lanes3(x, width):
    hi = x.astype(bf16).astype(f32)
    lo = x - hi
    zero = jnp.zeros((x.shape[0], width - x.shape[1]), f32)
    return jnp.concatenate([hi, zero, hi, zero, lo, zero], axis=1).astype(bf16)


def rows3(x):
    hi, lo = split(x)
    return jnp.concatenate([hi, lo, hi], axis=0)


N_OPS = 21


def kernel(*refs):
    sources, (out_d, out_a, out_h) = refs[:N_OPS], refs[N_OPS:N_OPS + 3]
    held = refs[N_OPS + 3:2 * N_OPS + 3]
    isem = refs[-1]
    loads = [pltpu.make_async_copy(a, b, isem.at[at]) for at, (a, b) in enumerate(zip(sources, held))]
    for load in loads:
        load.start()
    work(loads, *held, out_d, out_a, out_h, *refs[2 * N_OPS + 3:-1])


def work(
    loads,
    s0, dl, ad, model, geometry, normals, face_scale, derivative, lift, prolong, coarse, reg, observe,
    owner, local, child, neighbor, orient, send_face, pick, turn,
    out_d, out_a, out_h,
    tab, hot, dq, jump, hn, xl, fs, ltr, rst, c1,
    tr_s, tr_r, ag_s, ag_r, p1, p3, chot, new_d, new_a, lmat, order, packed, left,
    ssem, rsem, osem,
):
    region, wave = lax.axis_index("region"), lax.axis_index("wave")
    me = region * NW + wave
    core = lax.rem(wave, 2)
    barrier = pltpu.get_barrier_semaphore()

    def greet(there):
        pl.semaphore_signal(barrier, inc=1, device_id=there, device_id_type=MESH)

    def each(low, high, act):
        def one(i, c):
            act(i)
            return c

        lax.fori_loop(low, high, one, 0)

    half = lax.div(wave, 2)

    def level(i):
        return (region, lax.rem(wave + 2 * i, NW))

    def across(i):
        return (lax.rem(region + i, 4), wave)

    sibling = (region, wave + 1 - 2 * core)
    each(0, 16, lambda i: greet((region, lax.rem(wave + 2 * i + 1, NW))))
    each(1, 16, lambda i: greet(level(i)))
    each(1, 4, lambda i: greet(across(i)))

    def send(src, dst, at, there):
        pltpu.make_async_remote_copy(
            src_ref=src, dst_ref=dst, send_sem=ssem.at[at], recv_sem=rsem.at[at], device_id=there, device_id_type=MESH
        ).start()

    def wait(part, sem):
        pltpu.make_async_copy(part, part, sem).wait()

    for load in loads:
        load.wait()

    cs = jnp.concatenate([coarse[...], jnp.zeros((2, 32), f32)], axis=0)
    cst = jnp.concatenate([cs, jnp.zeros((32, 96), f32)], axis=1).T
    ag_s[...] = jnp.concatenate([cst[q * 8:q * 8 + 8, 0:32] for q in range(4)], axis=1)
    ag_r[pl.ds(half, 1), pl.ds(core, 1), pl.ds(region, 1)] = ag_s[...].reshape(1, 1, 1, 8, 128)

    u = (iota((ND, E), 0) == owner[...]).astype(f32).astype(bf16)
    ub = u.astype(f32)
    tri = (iota((E, E), 0) < iota((E, E), 1)).astype(f32).astype(bf16)
    before = jnp.sum(nn(u, tri) * ub, axis=0, keepdims=True).astype(i32)

    for k in range(3):
        c1[k * 40:(k + 1) * 40, :] = lanes3(below(derivative[k], 40), 48)
    c1[120:248, :] = pick[...]
    for s, ref in enumerate((s0, dl, ad)):
        for c in range(NF):
            sc = s * NF + c
            got = nn(c1[...], rows3(below(ref[c], 48)))
            dq[sc] = got[0:120]
            for f in range(4):
                span = slice(f * E, (f + 1) * E)
                tab[0, sc * 16:(sc + 1) * 16, span] = got[120 + f * 16:136 + f * 16].astype(bf16)
                tab[1, sc * 16:(sc + 1) * 16, span] = got[184 + f * 16:200 + f * 16].astype(bf16)

    turned = iota((8, 128), 1)
    turned = (turned & 31) * 4 + lax.shift_right_logical(turned, 5)
    chosen = jnp.broadcast_to(send_face[...].astype(f32), (8, 128))
    chosen = jnp.take_along_axis(chosen, turned, axis=1, mode="promise_in_bounds").astype(i32)
    pickt = (iota((OWN, 128), 0) == chosen[0:1]).astype(f32).astype(bf16)
    packed[...] = nn(tab[0, :, 0:OWN], pickt) + nn(tab[1, :, 0:OWN], pickt)
    for block, row in enumerate(MOVED):
        packed[block * 16 + 15:block * 16 + 16, :] = packed[row:row + 1, :]
    left[0:6, :] = packed[409:415, :]
    left[6:21, :] = packed[416:431, :]
    left[21:32, :] = jnp.zeros((11, 128), f32)
    rows_s = tr_s.reshape(13, NW, 128)
    for j in range(3):
        rows_s[j * 4:j * 4 + 4] = packed[j * 128:(j + 1) * 128, :].T.reshape(4, NW, 128)
    last = left[...].T
    rows_s[12] = jnp.concatenate([last[c * 32:(c + 1) * 32] for c in range(4)], axis=1)

    pl.semaphore_wait(barrier, 34)
    each(1, 4, lambda i: send(ag_s, ag_r.at[half, core, region], 1, across(i)))

    def send_trace(i):
        w = lax.rem(wave + i, NW)
        send(tr_s.at[:, pl.ds(w, 1)], tr_r.at[:, pl.ds(wave, 1)], 0, (region, w))

    each(1, NW, send_trace)
    tr_r[:, pl.ds(wave, 1)] = tr_s[:, pl.ds(wave, 1)]

    for f in range(4):
        named = neighbor[f:f + 1, :]
        far = OWN + (named & 3) * 32 + lax.shift_right_logical(named - OWN, 2)
        row = jnp.where(named < OWN, named, far).astype(i16)
        hot[:, f * E:(f + 1) * E] = jnp.where(
            iota((TAB, E), 0, i16) == row, jnp.ones((), bf16), jnp.zeros((), bf16)
        )

    wait(ag_r.at[0, 0, pl.ds(0, 3)], rsem.at[1])
    each(1, 16, lambda i: send(ag_r.at[half, core], ag_r.at[half, core], 4, level(i)))

    line = (lax.shift_right_logical(owner[...] & 31, 1) * 4 + lax.shift_right_logical(owner[...], 5)) * 8
    line = line + (local[...] & 7)
    for k in range(2):
        row = jnp.where((owner[...] & 1) == (core + k - 2 * core * k), line, -1).astype(i16)
        chot[k] = jnp.where(iota((512, E), 0, i16) == row, jnp.ones((), bf16), jnp.zeros((), bf16))

    for f in range(4):
        span = slice(f * E, (f + 1) * E)
        jump[:, span] = nn(tab[0, :, 0:OWN], hot[0:OWN, span]) + nn(tab[1, :, 0:OWN], hot[0:OWN, span])

    for f in range(4):
        span = slice(f * E, (f + 1) * E)
        h = 0.5 * face_scale[f:f + 1, :]
        for j in range(3):
            hn[j, :, span] = jnp.broadcast_to(h * normals[j, f:f + 1, :], (8, E))
        hn[3, :, span] = jnp.broadcast_to(h, (8, E))

    ltr[...] = jnp.zeros_like(ltr)
    for f in range(4):
        for m in range(15):
            ltr[f * 16 + m:f * 16 + m + 1, 0:NN] = lift[m, f:f + 1, :]
    lh, ll = split(ltr[...].T[0:40])
    lmat[...] = jnp.concatenate([lh.astype(f32), lh.astype(f32), ll.astype(f32)], axis=1).astype(bf16)

    for f in range(4):
        span = slice(f * E, (f + 1) * E)
        idx = jnp.full((16, E), 15, i32)
        for q in range(6):
            idx = jnp.where(orient[f:f + 1, :] == q, turn[:, q:q + 1], idx)
        order[:, span] = idx

    geo = [geometry[q:q + 1, :] for q in range(9)]

    def grad(sc, i):
        return sum(geo[3 * i + k] * dq[sc, k * 40:(k + 1) * 40, :] for k in range(3))

    for s in range(3):
        base = s * NF
        for i in range(3):
            fs[s, i] = sum(grad(base + 3 + STRESS[i][j], j) for j in range(3))
            fs[s, 3 + i] = grad(base + i, i)
        for at, (i, j) in enumerate(OFF):
            fs[s, 6 + at] = grad(base + j, i) + grad(base + i, j)

    mask = (iota((8, E), 0) == child[...]).astype(f32)
    pm = prolong[...].reshape(80, NN)
    pm40 = jnp.concatenate([pm, jnp.zeros((80, 5), f32)], axis=1)
    ph, pw = split(pm40)
    pm3 = jnp.concatenate([ph, ph, pw], axis=0)
    pm144 = lanes3(pm, 48)

    wait(tr_r.at[:, pl.ds(0, NW - 1)], rsem.at[0])
    rows_r = tr_r.reshape(13, NW, 128)
    for j in range(3):
        packed[j * 128:(j + 1) * 128, :] = rows_r[j * 4:j * 4 + 4].reshape(128, 128).T
    last = rows_r[12]
    left[...] = jnp.concatenate([last[:, c * 32:(c + 1) * 32] for c in range(4)], axis=0).T
    for row in (399, 415, 431):
        packed[row:row + 1, :] = jnp.zeros((1, 128), f32)
    for block, row in enumerate(MOVED):
        packed[row:row + 1, :] = packed[block * 16 + 15:block * 16 + 16, :]
    packed[409:415, :] = left[0:6, :]
    packed[416:431, :] = left[6:21, :]
    hi, lo = split(packed[...])
    tab[0, :, OWN:TAB] = hi
    tab[1, :, OWN:TAB] = lo
    for f in range(4):
        span = slice(f * E, (f + 1) * E)
        jump[:, span] += nn(tab[0, :, OWN:TAB], hot[OWN:TAB, span]) + nn(tab[1, :, OWN:TAB], hot[OWN:TAB, span])

    for f in range(4):
        span = slice(f * E, (f + 1) * E)
        idx = order[:, span]
        low = idx < 8
        idx = idx & 7
        ia, ib = idx[0:8], idx[8:16]
        for sc in range(27):
            a = jump[sc * 16:sc * 16 + 8, span]
            b = jump[sc * 16 + 8:sc * 16 + 16, span]
            own = tab[0, sc * 16:sc * 16 + 16, span].astype(f32) + tab[1, sc * 16:sc * 16 + 16, span].astype(f32)
            for t, ix in enumerate((ia, ib)):
                ga = jnp.take_along_axis(a, ix, axis=0, mode="promise_in_bounds")
                gb = jnp.take_along_axis(b, ix, axis=0, mode="promise_in_bounds")
                jump[sc * 16 + t * 8:sc * 16 + t * 8 + 8, span] = (
                    jnp.where(low[t * 8:t * 8 + 8], ga, gb) - own[t * 8:t * 8 + 8]
                )

    def terms(s):
        for f in range(4):
            span = slice(f * E, (f + 1) * E)
            n = [jnp.concatenate([hn[j, :, span]] * 2, axis=0) for j in range(4)]
            q = [jump[(s * NF + c) * 16:(s * NF + c) * 16 + 16, span] for c in range(NF)]
            chans = [sum(n[j] * q[3 + STRESS[i][j]] for j in range(3)) for i in range(3)]
            chans += [n[j] * q[j] for j in range(3)]
            chans += [n[i] * q[j] + n[j] * q[i] for i, j in OFF]
            if s > 0:
                chans += [n[3] * q[c] for c in range(NF)]
            for at, g in enumerate(chans):
                hi, lo = split(g)
                xl[at, f * 16:f * 16 + 16, :] = hi
                xl[at, 64 + f * 16:80 + f * 16, :] = lo
                xl[at, 128 + f * 16:144 + f * 16, :] = hi
        for at in range(9):
            fs[s, at] += nn(lmat[...], xl[at])
        if s > 0:
            for at in range(9, 18):
                fs[s, at] = nn(lmat[...], xl[at])

    terms(0)

    wait(ag_r.at[pl.ds(0, 15), 0], rsem.at[4])
    send(ag_r.at[:, pl.ds(core, 1)], ag_r.at[:, pl.ds(core, 1)], 2, sibling)

    def looked_up(k, at):
        hi, lo = split(ag_r[:, pl.ds(at, 1)].reshape(512, 128).T)
        return nn(hi, chot[k]) + nn(lo, chot[k])

    near = looked_up(0, core)

    terms(1)
    terms(2)

    m0, m1, m2 = (below(model[p], 40) for p in range(3))

    def lam(s):
        return fs[s, 3] + fs[s, 4] + fs[s, 5]

    def mu(s, k):
        return 2.0 * fs[s, 3 + k] if k < 3 else fs[s, 3 + k]

    for s, ref in ((1, dl), (2, ad)):
        lams = m1 * lam(s)
        for c in range(NF):
            grown = m0 * fs[s, c] if c < 3 else m2 * mu(s, c - 3)
            if 3 <= c < 6:
                grown = grown + lams
            fs[s, 9 + c] = below(ref[c], 40) + STEP * (grown + fs[s, 9 + c])
    lam0 = lam(0)

    wait(ag_r.at[:, pl.ds(0, 1)], rsem.at[2])
    found = jnp.where(
        lax.div(iota((128, E), 0), 32) == lax.shift_right_logical(local[...], 3), near + looked_up(1, 1 - core), 0.0
    )
    found = found[0:32] + found[32:64] + found[64:96] + found[96:128]
    fine = []
    for p in range(3):
        z = jnp.concatenate([mask * found[p * 10 + k:p * 10 + k + 1, :] for k in range(10)], axis=0)
        fine.append(tn(pm3, rows3(z)))

    obs = STEP * below(observe[...], 40)
    fine = [STEP * x for x in fine]
    lam1 = fine[1] * lam0
    gb = jnp.zeros((40, E), f32)
    tr = jnp.zeros((40, E), f32)
    gm = jnp.zeros((40, E), f32)
    for c in range(NF):
        if c < 3:
            term = fs[0, c]
            nd = fs[1, 9 + c] + fine[0] * term
        else:
            term = mu(0, c - 3)
            more = fine[2] * term
            if c < 6:
                more = more + lam1
            nd = fs[1, 9 + c] + more
        na = fs[2, 9 + c] + obs * nd
        new_d[c] = nd[0:NN]
        new_a[c] = na[0:NN]
        if c < 3:
            gb = gb + na * term
        else:
            gm = gm + na * term
            if c < 6:
                tr = tr + na
    stores = [pltpu.make_async_copy(new_d, out_d, osem.at[0]), pltpu.make_async_copy(new_a, out_a, osem.at[1])]
    for store in stores:
        store.start()
    fine_grad = (STEP * gb, STEP * tr * lam0, STEP * gm)

    rst[30:31, :] = local[...].astype(f32)
    rst[31:32, :] = jnp.zeros((1, E), f32)
    for p in range(3):
        r = nn(pm144, rows3(below(fine_grad[p], 48)))
        rst[p * 10:(p + 1) * 10, :] = jnp.sum(r.reshape(10, 8, E) * mask[None], axis=1)
    slot = lax.div(iota((128, E), 0), 32) == before
    wh, wl = split(jnp.where(slot, jnp.concatenate([rst[...]] * 4, axis=0), 0.0))
    p1.reshape(ND, 128)[...] = nt(u, wh) + nt(u, wl)

    def send_partial(i):
        d = lax.rem(me + i, ND)
        send(p1.at[d], p3.at[me], 3, (lax.div(d, NW), lax.rem(d, NW)))

    each(1, ND, send_partial)
    p3[pl.ds(me, 1)] = p1[pl.ds(me, 1)]
    place_of = lax.rem(iota((128, 128), 1), 32)
    spread = (iota((128, 128), 0) == iota((128, 128), 1) - place_of + 30).astype(f32).astype(bf16)
    same = lax.div(iota((128, 128), 0), 32) == lax.div(iota((128, 128), 1), 32)
    kept = reg[...] * coarse[...]
    wait(p3.at[pl.ds(0, ND - 1)], rsem.at[3])
    gh, gl = split(p3.reshape(ND, 128)[...])
    asked = (nn(gh, spread).astype(i32) == place_of).astype(f32).astype(bf16)
    total = jnp.where(same, tn(gh, asked) + tn(gl, asked), 0.0)
    total = total[0:32] + total[32:64] + total[64:96] + total[96:128]
    total = total[:, 0:32] + total[:, 32:64] + total[:, 64:96] + total[:, 96:128]
    out_h[...] = total[0:30] + kept

    wait(tr_s.at[:, pl.ds(0, NW - 1)], ssem.at[0])
    wait(ag_r.at[0, 0, pl.ds(0, 3)], ssem.at[1])
    wait(ag_r.at[pl.ds(0, 15), 0], ssem.at[4])
    wait(ag_r.at[:, pl.ds(0, 1)], ssem.at[2])
    wait(p1.at[pl.ds(0, ND - 1)], ssem.at[3])
    for store in stores:
        store.wait()


def place(*refs):
    isem, osem = refs[-2:]
    loads = [pltpu.make_async_copy(refs[at], refs[6 + at], isem.at[at]) for at in range(3)]
    stores = [pltpu.make_async_copy(refs[6 + at], refs[3 + at], osem.at[at]) for at in range(3)]
    for load in loads:
        load.start()
    for load, store in zip(loads, stores):
        load.wait()
        store.start()
    for store in stores:
        store.wait()


def body(
    state0, delta, adjoint, model, geometry, normals, face_scale, derivative, lift, prolong, coarse_step, reg_weight,
    observe, owner, coarse_local, child, neighbor, orient, send_face,
):
    pick, turn = constants()
    ops = (
        state0, delta, adjoint, model, geometry, normals, face_scale, derivative,
        lift.transpose(2, 0, 1), prolong.transpose(2, 0, 1), coarse_step, reg_weight, observe,
        owner.reshape(1, E), coarse_local.reshape(1, E), child.reshape(1, E), neighbor, orient, send_face.reshape(1, 128),
        jnp.asarray(pick, bf16), jnp.asarray(turn),
    )
    vmem = pl.BlockSpec(memory_space=pltpu.VMEM)
    anywhere = pl.BlockSpec(memory_space=pl.ANY)
    hbm = pl.BlockSpec(memory_space=pltpu.HBM)
    row = pltpu.VMEM((ND, 1, 128), f32)
    results = (
        jax.ShapeDtypeStruct((NF, NN, E), f32),
        jax.ShapeDtypeStruct((NF, NN, E), f32),
        jax.ShapeDtypeStruct((30, 32), f32),
    )
    found = pl.pallas_call(
        kernel,
        out_shape=results,
        in_specs=[hbm] * len(ops),
        out_specs=(hbm, hbm, vmem),
        scratch_shapes=[
            *(pltpu.VMEM(op.shape, op.dtype) for op in ops),
            pltpu.VMEM((2, ROWS, TAB), bf16),
            pltpu.VMEM((TAB, OWN), bf16),
            pltpu.VMEM((27, 120, E), f32),
            pltpu.VMEM((ROWS, OWN), f32),
            pltpu.VMEM((4, 8, OWN), f32),
            pltpu.VMEM((18, 192, E), bf16),
            pltpu.VMEM((3, 18, 40, E), f32),
            pltpu.VMEM((64, 128), f32),
            pltpu.VMEM((32, E), f32),
            pltpu.VMEM((248, 144), bf16),
            pltpu.VMEM((13, NW, 1, 128), f32),
            pltpu.VMEM((13, NW, 1, 128), f32),
            pltpu.VMEM((8, 128), f32),
            pltpu.VMEM((16, 2, 4, 8, 128), f32),
            row, row,
            pltpu.VMEM((2, 512, E), bf16),
            pltpu.VMEM((NF, NN, E), f32),
            pltpu.VMEM((NF, NN, E), f32),
            pltpu.VMEM((40, 192), bf16),
            pltpu.VMEM((16, OWN), i32),
            pltpu.VMEM((ROWS, 128), f32),
            pltpu.VMEM((32, 128), f32),
            pltpu.SemaphoreType.DMA((5,)),
            pltpu.SemaphoreType.DMA((5,)),
            pltpu.SemaphoreType.DMA((2,)),
            pltpu.SemaphoreType.DMA((N_OPS,)),
        ],
        compiler_params=pltpu.CompilerParams(
            collective_id=0, has_side_effects=True, vmem_limit_bytes=60 * 1024 * 1024
        ),
    )(*ops)
    return pl.pallas_call(
        place,
        out_shape=results,
        in_specs=[anywhere] * 3,
        out_specs=(hbm, hbm, hbm),
        scratch_shapes=[
            *(pltpu.VMEM(r.shape, r.dtype) for r in results),
            pltpu.SemaphoreType.DMA((3,)),
            pltpu.SemaphoreType.DMA((3,)),
        ],
        compiler_params=pltpu.CompilerParams(vmem_limit_bytes=60 * 1024 * 1024),
    )(*found)


def solution(mesh):
    both = ("region", "wave")
    placed = (
        P(None, None, both), P(None, None, both), P(None, None, both), P(None, None, both), P(None, both),
        P(None, None, both), P(None, both), P(), P(), P(), P(None, both), P(None, both), P(None, both),
        P(both, None), P(both), P(both), P(None, both), P(None, both), P(both),
    )
    return jax.shard_map(
        body, mesh=mesh, in_specs=placed,
        out_specs=(P(None, None, both), P(None, None, both), P(None, both)), check_vma=False,
    )
```
